256 devices in a mesh: member: 4 (over y_lo, core), grid: 64 (over y_hi, z, x).
Axes of the slice: x: 4, y: 4 (y_hi: 2, y_lo: 2; y = y_hi * 2 + y_lo), z: 8, core: 2. Of those that a mesh axis runs over, the one named last changes fastest.
Arguments:
- mesh_features: float32 [8, 2048, 512], P('member', 'grid'), may hold values from -6 to 6
- grid_features: float32 [8, 32768, 512], P('member', 'grid'), may hold values from -6 to 6
- targets: float32 [100, 32768], P(None, 'grid'), may hold values from -12 to 12
- edges: int32 [4, 32768], P(None, 'grid'), may hold values from 0 to 2047, as said below
- src_weight: float32 [512, 512], replicated, may hold values from -0.25 to 0.25
- dst_weight: float32 [512, 512], replicated, may hold values from -0.25 to 0.25
- output_weight: float32 [512, 100], replicated, may hold values from -0.25 to 0.25
Outputs:
- loss: float32 [], replicated
- grid_grad: float32 [8, 32768, 512], P('member', 'grid')
- mesh_grad: float32 [8, 2048, 512], P('member', 'grid')
- src_grad: float32 [512, 512], replicated
- dst_grad: float32 [512, 512], replicated
- out_grad: float32 [512, 100], replicated
The draws below stay inside these ranges and needn't reach their ends.
Inputs may be any that keep to these rules, and one draw needn't show every extreme that they name: `edges`: the mesh nodes of grid point p lie among the nodes (s - 1) * 32 to (s + 2) * 32 - 1, with s = p // 512.
All inputs are finite; a program needn't handle non-finite values.
Results may differ from the reference program's by a relative error of at most 0.0003.
Values sent between devices are 32-bit elements; how exact they have to be, the bound alone decides.
No kernel may reach another device: no remote copies, remote signals or barrier semaphores. Data moves between devices by JAX's collectives and lax.ppermute only.
A program may use at most 64 MiB of HBM per device.

```python
import jax
import jax.numpy as jnp
from jax import lax

W = 512
VARS = 100
DEG = 4
GP_DEV = 512
MESH_DEV = 32
MEMBERS = 8
POINTS = 32768
MESH = 2048


def draw_edges(key, part):
    key = jax.random.fold_in(key, 11)
    key_side, key_node = jax.random.split(key)
    slabs = POINTS // GP_DEV
    owner = (jnp.arange(POINTS, dtype=jnp.int32) // GP_DEV)[None, :]
    side = jax.random.randint(key_side, (DEG, POINTS), -1, 2)
    target = jnp.clip(owner + side, 0, slabs - 1)
    node = jax.random.randint(key_node, (DEG, POINTS), 0, MESH_DEV)
    return (target * MESH_DEV + node).astype(jnp.int32)


def block_scale(key, shape, cuts, low, high):
    def one(position, blocks):
        draws = jax.random.uniform(jax.random.fold_in(jax.random.fold_in(key, 6), position), (blocks,), jnp.float32, low / len(cuts), high / len(cuts))
        return jnp.repeat(jnp.exp(draws), shape[position] // blocks).reshape((-1,) + (1,) * (len(shape) - position - 1))

    factor_of = one(*cuts[0])
    for cut in cuts[1:]:
        factor_of = factor_of * one(*cut)
    return factor_of


def noise(stream_key, shape, deviation, most, shards=(), kind=jnp.bfloat16):
    result = jax.random.normal(stream_key, shape, jnp.float32) * deviation
    if len(shards) > 0:
        result = block_scale(stream_key, shape, shards, -0.22, 0.18) * result
    return jnp.clip(result, min=-most, max=most).astype(kind)


def setup_inputs(seed: int = 0) -> dict:
    key_list = jax.random.split(jax.random.key(seed), 8)
    return {
        "mesh_features": noise(key_list[0], (MEMBERS, MESH, W), 1.0, 6.0, ((0, 4), (1, 64)), jnp.float32),
        "grid_features": noise(key_list[1], (MEMBERS, POINTS, W), 1.0, 6.0, ((0, 4), (1, 64)), jnp.float32),
        "targets": noise(key_list[2], (VARS, POINTS), 2.0, 12.0, ((1, 64),), jnp.float32),
        "edges": draw_edges(jax.random.fold_in(key_list[7], 71), 0),
        "src_weight": noise(key_list[4], (W, W), W ** -0.5, 0.25, (), jnp.float32),
        "dst_weight": noise(key_list[5], (W, W), W ** -0.5, 0.25, (), jnp.float32),
        "output_weight": noise(key_list[6], (W, VARS), W ** -0.5, 0.25, (), jnp.float32),
    }


alpha_fair = 0.95
smoothing = 0.1

def smooth_abs(value):
    return jnp.sqrt(value * value + smoothing * smoothing)

def silu_slope(value):
    sigma = jax.nn.sigmoid(value)
    return sigma * (1.0 + value * (1.0 - sigma))

def score_terms_list(own_members, all_members, truth):
    count = all_members.shape[0]
    spread = (1.0 - alpha_fair) / count
    factor = (1.0 - spread) / (count * (count - 1))
    error = own_members - truth[None]
    dist_truth = smooth_abs(error)
    pair_sum = jnp.zeros_like(own_members)
    pair_slope = jnp.zeros_like(own_members)
    for other in range(count):
        differ = own_members - all_members[other][None]
        distance = smooth_abs(differ)
        pair_sum = pair_sum + (distance - smoothing)
        pair_slope = pair_slope + differ / distance
    summed_loss = jnp.sum(dist_truth) / count - 0.5 * factor * jnp.sum(pair_sum)
    gradient_result = error / dist_truth / count - factor * pair_slope
    return (gradient_result, summed_loss)

def reference(mesh_features, grid_features, targets, edges, src_weight, dst_weight, output_weight):
    highest_precision = lax.Precision.HIGHEST

    def decode(mesh_m, grid_m):
        projected = jnp.dot(mesh_m, src_weight, precision=highest_precision)
        query = jnp.dot(grid_m, dst_weight, precision=highest_precision)
        preact = projected[edges] + query[None]
        summed_values = lax.optimization_barrier(jnp.sum(jax.nn.silu(preact), axis=0))
        return (preact, summed_values)

    def forward_decode(member_index):
        preact, summed_values = decode(member_index[0], member_index[1])
        return jnp.dot(output_weight.T, summed_values.T, precision=highest_precision)
    predicted_fields = lax.map(forward_decode, (mesh_features, grid_features))
    gradient_result, summed_loss = score_terms_list(predicted_fields, predicted_fields, targets)

    def backward(member_index):
        mesh_m, grid_m, grad_m = member_index
        preact, summed_values = decode(mesh_m, grid_m)
        grad_summed = jnp.dot(grad_m.T, output_weight.T, precision=highest_precision)
        grad_pre = grad_summed[None] * silu_slope(preact)
        grad_query = lax.optimization_barrier(jnp.sum(grad_pre, axis=0))
        grad_proj = jnp.zeros((MESH, W), jnp.float32).at[edges].add(grad_pre)
        return (jnp.dot(grad_query, dst_weight.T, precision=highest_precision), jnp.dot(grad_proj, src_weight.T, precision=highest_precision), jnp.dot(mesh_m.T, grad_proj, precision=highest_precision), jnp.dot(grid_m.T, grad_query, precision=highest_precision), jnp.dot(summed_values.T, grad_m.T, precision=highest_precision))
    grid_grad, mesh_grad, src_parts, dst_parts, out_parts = lax.map(backward, (mesh_features, grid_features, gradient_result))
    scale = 1.0 / jnp.sqrt(jnp.float32(MEMBERS * POINTS))
    loss = summed_loss / (POINTS * VARS)
    return (loss, grid_grad, mesh_grad, lax.optimization_barrier(jnp.sum(src_parts, axis=0)) * scale, lax.optimization_barrier(jnp.sum(dst_parts, axis=0)) * scale, lax.optimization_barrier(jnp.sum(out_parts, axis=0)) * scale)
```

```python
import functools

import jax
import jax.numpy as jnp
from jax import lax
from jax.experimental import pallas as pl
from jax.experimental.pallas import tpu as pltpu
from jax.sharding import PartitionSpec as P

alpha_fair = 0.95
smoothing = 0.1
axes = ("member", "grid")
vmem_limit = 56 * 1024 * 1024
f32 = jnp.float32
bf16 = jnp.bfloat16
interpret = False


def place_of(member, grid):
    return {
        "core": member & 1,
        "y": ((grid >> 5) << 1) | (member >> 1),
        "z": (grid >> 2) & 7,
        "x": grid & 3,
    }


def exchange(change):
    pairs = []
    for member in range(4):
        for grid in range(64):
            place = place_of(member, grid)
            place = {**place, **change(place)}
            member_to = ((place["y"] & 1) << 1) | place["core"]
            grid_to = ((place["y"] >> 1) << 5) | (place["z"] << 2) | place["x"]
            pairs.append((member * 64 + grid, member_to * 64 + grid_to))
    return pairs


swap_core = exchange(lambda c: {"core": c["core"] ^ 1})
first_axis = [
    exchange(lambda c, k=k: {"x": c["x"] ^ k} if c["core"] == 0 else {"y": c["y"] ^ k}) for k in range(4)
]
second_axis = [
    exchange(lambda c, k=k: {"y": c["y"] ^ k} if c["core"] == 0 else {"x": c["x"] ^ k}) for k in range(4)
]
along_z = [exchange(lambda c, k=k: {"z": c["z"] ^ k}) for k in range(8)]


def send(value, pairs):
    return lax.ppermute(value, axes, pairs)


def split(value):
    high = value.astype(bf16)
    return high, (value - high.astype(f32)).astype(bf16)


def dot3(left, right, dims):
    def one(a, b):
        return lax.dot_general(a, b, (dims, ((), ())), preferred_element_type=f32)

    return one(left[0], right[0]) + (one(left[0], right[1]) + one(left[1], right[0]))


NN = ((1,), (0,))
NT = ((1,), (1,))
TN = ((0,), (0,))


def forward_kernel(points, me, query, edges, before, own, after, src_weight, out_weight,
                   slope, summed, part0, part1, part2, part3, nodes, fields):
    member, tile = pl.program_id(0), pl.program_id(1)
    tiles = pl.num_programs(1)
    rows = own.shape[1]

    @pl.when((member == 0) & (tile == 0))
    def _():
        nodes[...] = jnp.zeros_like(nodes)
        weight = split(src_weight[...])
        for n in range(own.shape[0]):
            ext = jnp.concatenate([before[n], own[n], after[n]], axis=0)
            high, low = split(dot3(split(ext), weight, NN))
            nodes[n, 0 : 3 * rows] = high
            nodes[n, 128 : 128 + 3 * rows] = low

    local = edges[...] - (me[1] - 1) * rows
    columns = lax.broadcasted_iota(jnp.int32, (points, 256), 1) & 127
    total = None
    for k in range(4):
        hot = jnp.where(local[:, k : k + 1] == columns, 1.0, 0.0).astype(bf16)
        value = query[0] + jnp.dot(hot, nodes[member], preferred_element_type=f32)
        sigma = 0.5 * jnp.tanh(0.5 * value) + 0.5
        active = value * sigma
        slope[0, k] = sigma + active * (1.0 - sigma)
        total = active if total is None else total + active
    summed[0] = total
    weight = split(out_weight[...])
    fields[:, pl.ds(pl.multiple_of(tile * points, 128), points)] = dot3(weight, split(total), NT)

    @pl.when(tile == tiles - 1)
    def _():
        for k, part in enumerate((part0, part1, part2, part3)):
            part[member] = fields[:, pl.ds(pl.multiple_of((me[0] ^ k) * 128, 128), 128)]


def score_kernel(count_vars, me, part0, part1, part2, part3, targets, out0, out1, out2, out3, loss):
    parts, outs = (part0, part1, part2, part3), (out0, out1, out2, out3)
    count = 8
    spread = (1.0 - alpha_fair) / count
    factor = (1.0 - spread) / (count * (count - 1))
    rows = targets.shape[0]
    near = jnp.zeros((8, 128), f32)
    far = jnp.zeros((8, 128), f32)
    for block in range(rows // 8):
        at = pl.ds(block * 8, 8)
        real = block * 8 + lax.broadcasted_iota(jnp.int32, (8, 128), 0) < count_vars
        truth = targets[at]
        fields = [parts[j // 2][j % 2, at] for j in range(count)]
        slopes, dist_sum = [], None
        for field in fields:
            error = field - truth
            square = error * error + smoothing * smoothing
            inverse = lax.rsqrt(square)
            dist = square * inverse
            dist_sum = dist if dist_sum is None else dist_sum + dist
            slopes.append(error * inverse * (1.0 / count))
        pair_sum = None
        pairs = [None] * count
        for j in range(count):
            for k in range(j + 1, count):
                differ = fields[j] - fields[k]
                square = differ * differ + smoothing * smoothing
                inverse = lax.rsqrt(square)
                dist = square * inverse - smoothing
                pair_sum = dist if pair_sum is None else pair_sum + dist
                term = differ * inverse
                pairs[j] = term if pairs[j] is None else pairs[j] + term
                pairs[k] = -term if pairs[k] is None else pairs[k] - term
        near += jnp.where(real, dist_sum, 0.0)
        far += jnp.where(real, pair_sum, 0.0)
        for j in range(count):
            outs[j // 2][j % 2, at] = slopes[j] - factor * pairs[j]
    loss[...] = near * (1.0 / count) - factor * far


def backward_kernel(points, scale, loss_scale, me, part0, part1, part2, part3, loss, slope, summed, features,
                    edges, before, own, after, out_weight,
                    grad_query, grad_ext, keep, away, slopes, sums):
    member, tile = pl.program_id(0), pl.program_id(1)
    members, tiles = pl.num_programs(0), pl.num_programs(1)
    rows = own.shape[1]
    width = features.shape[2]
    vars_rows = out_weight.shape[0]

    @pl.when((member == 0) & (tile == 0))
    def _():
        sums[...] = jnp.zeros_like(sums)
        grad_ext[...] = jnp.zeros_like(grad_ext)
        for k, part in enumerate((part0, part1, part2, part3)):
            for n in range(2):
                slopes[n, :, pl.ds(pl.multiple_of((me[0] ^ k) * 128, 128), 128)] = part[n]

    here = split(slopes[member, :, pl.ds(pl.multiple_of(tile * points, 128), points)])
    back = dot3(here, split(out_weight[...]), TN)
    sums[2 * width : 2 * width + vars_rows] += dot3(here, split(summed[0]), NN)
    local = edges[...] - (me[1] - 1) * rows
    nodes = lax.broadcasted_iota(jnp.int32, (3 * rows, points), 0)
    scattered = None
    slope_sum = None
    for k in range(4):
        hot = jnp.where(local[k : k + 1] == nodes, 1.0, 0.0).astype(bf16)
        slope_k = slope[0, k]
        slope_sum = slope_k if slope_sum is None else slope_sum + slope_k
        high, low = split(back * slope_k)
        term = jnp.dot(hot, high, preferred_element_type=f32) + jnp.dot(
            hot, low, preferred_element_type=f32
        )
        scattered = term if scattered is None else scattered + term
    grad_ext[member] += scattered
    into_query = back * slope_sum
    grad_query[0] = into_query
    sums[width : 2 * width] += dot3(split(features[0]), split(into_query), TN)

    @pl.when((member == members - 1) & (tile == tiles - 1))
    def _():
        ext = jnp.concatenate([side[n] for n in range(2) for side in (before, own, after)], axis=0)
        grads = jnp.concatenate([grad_ext[0], grad_ext[1]], axis=0)
        sums[0:width] = dot3(split(ext), split(grads), TN)
        end = 2 * width + vars_rows
        sums[end : end + 8] = jnp.concatenate(
            [loss[...] * (loss_scale / scale), jnp.zeros((8, width - 128), f32)], axis=1
        )
        for j in range(16):
            for out, core, order in ((keep, me[2], me[3]), (away, 1 - me[2], me[4])):
                chunk = core * 16 + (j ^ order)
                at = pl.ds(pl.multiple_of((chunk >> 1) * 72, 8), 72)
                lanes = pl.ds(pl.multiple_of((chunk & 1) * 256, 128), 256)
                out[j] = sums[at, lanes] * scale


def finish_kernel(me, mine, other, src_grad, dst_grad, out_grad, loss, sums):
    width = src_grad.shape[0]
    for j in range(16):
        for part, core, order in ((mine, me[2], me[3]), (other, 1 - me[2], me[4])):
            chunk = core * 16 + (j ^ order)
            at = pl.ds(pl.multiple_of((chunk >> 1) * 72, 8), 72)
            lanes = pl.ds(pl.multiple_of((chunk & 1) * 256, 128), 256)
            sums[at, lanes] = part[j]
    src_grad[...] = sums[0:width]
    dst_grad[...] = sums[width : 2 * width]
    rows = 128
    out_grad[...] = sums[2 * width : 2 * width + rows].T[:, : out_grad.shape[1]]
    end = 2 * width + 104
    loss[...] = sums[end : end + 8, 0:128]


def whole(shape=None):
    return pl.BlockSpec(memory_space=pltpu.VMEM)


def params(dims):
    return pltpu.CompilerParams(dimension_semantics=("arbitrary",) * dims, vmem_limit_bytes=vmem_limit)


def all_reduce(keep, away):
    total = keep + send(away, swap_core)
    for group, size in ((first_axis, 4), (second_axis, 1)):
        parts = [send(total[k * size : (k + 1) * size], group[k]) for k in (1, 2, 3)]
        total = total[:size] + parts[0] + parts[1] + parts[2]
    parts = [send(total, along_z[k]) for k in (1, 2, 3)]
    total = total + parts[0] + parts[1] + parts[2]
    total = total + send(total, along_z[4])
    for group in (second_axis, first_axis):
        total = jnp.concatenate([total] + [send(total, group[k]) for k in (1, 2, 3)], axis=0)
    return total, send(total, swap_core)


def body(mesh_features, grid_features, targets, edges, src_weight, dst_weight, output_weight):
    members, rows, width = mesh_features.shape
    points = grid_features.shape[1]
    count_vars = targets.shape[0]
    var_rows = -(-count_vars // 8) * 8
    slabs = lax.axis_size("grid")
    member, grid = lax.axis_index("member"), lax.axis_index("grid")
    place = place_of(member, grid)
    x_then_y = place["x"] * 4 + place["y"]
    y_then_x = place["y"] * 4 + place["x"]
    straight = place["core"] == 0
    me = jnp.stack([
        member,
        grid,
        place["core"],
        jnp.where(straight, x_then_y, y_then_x),
        jnp.where(straight, y_then_x, x_then_y),
    ]).astype(jnp.int32)

    up = [(i, i + 1) for i in range(slabs - 1)]
    down = [(j, i) for i, j in up]
    before = lax.ppermute(mesh_features, "grid", up)
    after = lax.ppermute(mesh_features, "grid", down)
    query = jnp.einsum("npw,wu->npu", grid_features, dst_weight, precision=lax.Precision.HIGH)
    edges_t = edges.T
    out_weight = jnp.pad(output_weight.T, ((0, var_rows - count_vars), (0, 0)))
    targets = jnp.pad(targets, ((0, var_rows - count_vars), (0, 0)))

    tile = 256
    tiles = points // tile
    part_shape = jax.ShapeDtypeStruct((members, var_rows, 128), f32)
    slope, summed, *parts = pl.pallas_call(
        functools.partial(forward_kernel, tile),
        grid_spec=pltpu.PrefetchScalarGridSpec(
            num_scalar_prefetch=1,
            grid=(members, tiles),
            in_specs=[
                pl.BlockSpec((1, tile, width), lambda n, t, me: (n, t, 0)),
                pl.BlockSpec((tile, 4), lambda n, t, me: (t, 0)),
                whole(), whole(), whole(), whole(), whole(),
            ],
            out_specs=[
                pl.BlockSpec((1, 4, tile, width), lambda n, t, me: (n, 0, t, 0)),
                pl.BlockSpec((1, tile, width), lambda n, t, me: (n, t, 0)),
            ] + [whole()] * 4,
            scratch_shapes=[
                pltpu.VMEM((members, 256, width), bf16),
                pltpu.VMEM((var_rows, points), f32),
            ],
        ),
        out_shape=[
            jax.ShapeDtypeStruct((members, 4, points, width), f32),
            jax.ShapeDtypeStruct((members, points, width), f32),
        ] + [part_shape] * 4,
        compiler_params=params(2),
        name="forward",
        interpret=interpret,
    )(me, query, edges_t, before, mesh_features, after, src_weight, out_weight)

    to_peer = [[(i, i ^ k) for i in range(4)] for k in range(4)]
    parts = [parts[0]] + [lax.ppermute(parts[k], "member", to_peer[k]) for k in (1, 2, 3)]
    *slopes, loss = pl.pallas_call(
        functools.partial(score_kernel, count_vars),
        grid_spec=pltpu.PrefetchScalarGridSpec(
            num_scalar_prefetch=1,
            grid=(1,),
            in_specs=[whole()] * 4 + [pl.BlockSpec((var_rows, 128), lambda i, me: (0, me[0]))],
            out_specs=[whole()] * 5,
        ),
        out_shape=[part_shape] * 4 + [jax.ShapeDtypeStruct((8, 128), f32)],
        compiler_params=params(1),
        name="score",
        interpret=interpret,
    )(me, *parts, targets)
    slopes = [slopes[0]] + [lax.ppermute(slopes[k], "member", to_peer[k]) for k in (1, 2, 3)]

    total_members = lax.axis_size("member") * members
    scale = 1.0 / (total_members * points * slabs) ** 0.5
    loss_scale = 1.0 / (points * slabs * count_vars)
    chunks = jax.ShapeDtypeStruct((16, 72, 256), f32)
    grad_query, grad_ext, keep, away = pl.pallas_call(
        functools.partial(backward_kernel, tile, scale, loss_scale),
        grid_spec=pltpu.PrefetchScalarGridSpec(
            num_scalar_prefetch=1,
            grid=(members, tiles),
            in_specs=[whole()] * 5 + [
                pl.BlockSpec((1, 4, tile, width), lambda n, t, me: (n, 0, t, 0)),
                pl.BlockSpec((1, tile, width), lambda n, t, me: (n, t, 0)),
                pl.BlockSpec((1, tile, width), lambda n, t, me: (n, t, 0)),
                pl.BlockSpec((4, tile), lambda n, t, me: (0, t)),
                whole(), whole(), whole(), whole(),
            ],
            out_specs=[
                pl.BlockSpec((1, tile, width), lambda n, t, me: (n, t, 0)),
                whole(), whole(), whole(),
            ],
            scratch_shapes=[
                pltpu.VMEM((members, var_rows, points), f32),
                pltpu.VMEM((1152, width), f32),
            ],
        ),
        out_shape=[
            jax.ShapeDtypeStruct((members, points, width), f32),
            jax.ShapeDtypeStruct((members, 3 * rows, width), f32),
            chunks,
            chunks,
        ],
        compiler_params=params(2),
        name="backward",
        interpret=interpret,
    )(me, *slopes, loss, slope, summed, grid_features, edges, before, mesh_features, after, out_weight)

    mine, other = all_reduce(keep, away)
    from_prev = lax.ppermute(grad_ext[:, 2 * rows :], "grid", up)
    from_next = lax.ppermute(grad_ext[:, :rows], "grid", down)
    grid_grad = jnp.einsum("npu,wu->npw", grad_query, dst_weight, precision=lax.Precision.HIGH)
    grad_proj = grad_ext[:, rows : 2 * rows] + from_prev + from_next
    mesh_grad = jnp.einsum("nru,wu->nrw", grad_proj, src_weight, precision=lax.Precision.HIGH)

    square = jax.ShapeDtypeStruct((width, width), f32)
    src_grad, dst_grad, out_grad, loss = pl.pallas_call(
        finish_kernel,
        grid_spec=pltpu.PrefetchScalarGridSpec(
            num_scalar_prefetch=1,
            grid=(1,),
            in_specs=[whole()] * 2,
            out_specs=[whole()] * 4,
            scratch_shapes=[pltpu.VMEM((1152, width), f32)],
        ),
        out_shape=[
            square,
            square,
            jax.ShapeDtypeStruct((width, count_vars), f32),
            jax.ShapeDtypeStruct((8, 128), f32),
        ],
        compiler_params=params(1),
        name="finish",
        interpret=interpret,
    )(me, mine, other)
    return (jnp.sum(loss), grid_grad, mesh_grad, src_grad, dst_grad, out_grad)


def solution(mesh):
    placed = (
        P("member", "grid", None),
        P("member", "grid", None),
        P(None, "grid"),
        P(None, "grid"),
        P(),
        P(),
        P(),
    )
    return jax.shard_map(
        body,
        mesh=mesh,
        in_specs=placed,
        out_specs=(P(), P("member", "grid", None), P("member", "grid", None), P(), P(), P()),
        check_vma=False,
    )
```

```python
import functools

import jax
import jax.numpy as jnp
from jax import lax
from jax.experimental import pallas as pl
from jax.experimental.pallas import tpu as pltpu
from jax.sharding import PartitionSpec as P

alpha_fair = 0.95
smoothing = 0.1
axes = ("member", "grid")
vmem_limit = 24 * 1024 * 1024
f32 = jnp.float32
bf16 = jnp.bfloat16
interpret = False


def place_of(member, grid):
    return {
        "core": member & 1,
        "y": ((grid >> 5) << 1) | (member >> 1),
        "z": (grid >> 2) & 7,
        "x": grid & 3,
    }


def exchange(change):
    pairs = []
    for member in range(4):
        for grid in range(64):
            place = place_of(member, grid)
            place = {**place, **change(place)}
            member_to = ((place["y"] & 1) << 1) | place["core"]
            grid_to = ((place["y"] >> 1) << 5) | (place["z"] << 2) | place["x"]
            pairs.append((member * 64 + grid, member_to * 64 + grid_to))
    return pairs


swap_core = exchange(lambda c: {"core": c["core"] ^ 1})
first_axis = [
    exchange(lambda c, k=k: {"x": c["x"] ^ k} if c["core"] == 0 else {"y": c["y"] ^ k}) for k in range(4)
]
second_axis = [
    exchange(lambda c, k=k: {"y": c["y"] ^ k} if c["core"] == 0 else {"x": c["x"] ^ k}) for k in range(4)
]
along_z = [exchange(lambda c, k=k: {"z": c["z"] ^ k}) for k in range(8)]


def send(value, pairs):
    return lax.ppermute(value, axes, pairs)


def split(value):
    high = value.astype(bf16)
    return high, (value - high.astype(f32)).astype(bf16)


def dot3(left, right, dims):
    def one(a, b):
        return lax.dot_general(a, b, (dims, ((), ())), preferred_element_type=f32)

    return one(left[0], right[0]) + (one(left[0], right[1]) + one(left[1], right[0]))


NN = ((1,), (0,))
NT = ((1,), (1,))
TN = ((0,), (0,))


def query_kernel(features, weight, query, high, low):
    @pl.when(pl.program_id(0) == 0)
    def _():
        high[...], low[...] = split(0.5 * weight[...])

    query[0] = dot3(split(features[0]), (high[...], low[...]), NN)


def forward_kernel(points, me, query, edges, before, own, after, src_weight, out_weight,
                   slope, summed, part0, part1, part2, part3, nodes, fields):
    member, tile = pl.program_id(0), pl.program_id(1)
    tiles = pl.num_programs(1)
    rows = own.shape[1]

    @pl.when((member == 0) & (tile == 0))
    def _():
        nodes[...] = jnp.zeros_like(nodes)
        weight = split(0.5 * src_weight[...])
        for n in range(own.shape[0]):
            ext = jnp.concatenate([before[n], own[n], after[n]], axis=0)
            high, low = split(dot3(split(ext), weight, NN))
            nodes[n, 0 : 3 * rows] = high
            nodes[n, 128 : 128 + 3 * rows] = low

    local = edges[...] - (me[1] - 1) * rows
    columns = lax.broadcasted_iota(jnp.int32, (points, 256), 1) & 127
    total = None
    for k in range(4):
        hot = jnp.where(local[:, k : k + 1] == columns, 1.0, 0.0).astype(bf16)
        half = query[0] + jnp.dot(hot, nodes[member], preferred_element_type=f32)
        curve = jnp.tanh(half)
        active = half * curve + half
        curve = 0.5 * curve
        slope[0, k] = (curve + 0.5) + active * (0.5 - curve)
        total = active if total is None else total + active
    summed[0] = total
    weight = split(out_weight[...])
    fields[:, pl.ds(pl.multiple_of(tile * points, 128), points)] = dot3(weight, split(total), NT)

    @pl.when(tile == tiles - 1)
    def _():
        for k, part in enumerate((part0, part1, part2, part3)):
            part[member] = fields[:, pl.ds(pl.multiple_of((me[0] ^ k) * 128, 128), 128)]


def score_kernel(count_vars, me, part0, part1, part2, part3, targets, out0, out1, out2, out3, loss):
    parts, outs = (part0, part1, part2, part3), (out0, out1, out2, out3)
    count = 8
    spread = (1.0 - alpha_fair) / count
    factor = (1.0 - spread) / (count * (count - 1))
    rows = targets.shape[0]
    near = jnp.zeros((8, 128), f32)
    far = jnp.zeros((8, 128), f32)
    for block in range(rows // 8):
        at = pl.ds(block * 8, 8)
        real = block * 8 + lax.broadcasted_iota(jnp.int32, (8, 128), 0) < count_vars
        truth = targets[at]
        fields = [parts[j // 2][j % 2, at] for j in range(count)]
        slopes, dist_sum = [], None
        for field in fields:
            error = field - truth
            square = error * error + smoothing * smoothing
            inverse = lax.rsqrt(square)
            dist = square * inverse
            dist_sum = dist if dist_sum is None else dist_sum + dist
            slopes.append(error * inverse * (1.0 / count))
        pair_sum = None
        pairs = [None] * count
        for j in range(count):
            for k in range(j + 1, count):
                differ = fields[j] - fields[k]
                square = differ * differ + smoothing * smoothing
                inverse = lax.rsqrt(square)
                dist = square * inverse - smoothing
                pair_sum = dist if pair_sum is None else pair_sum + dist
                term = differ * inverse
                pairs[j] = term if pairs[j] is None else pairs[j] + term
                pairs[k] = -term if pairs[k] is None else pairs[k] - term
        near += jnp.where(real, dist_sum, 0.0)
        far += jnp.where(real, pair_sum, 0.0)
        for j in range(count):
            outs[j // 2][j % 2, at] = slopes[j] - factor * pairs[j]
    loss[...] = near * (1.0 / count) - factor * far


def backward_kernel(points, scale, loss_scale, me, part0, part1, part2, part3, loss, slope, summed, features,
                    edges, before, own, after, out_weight,
                    grad_query, lower, middle, upper, keep, away, grad_ext, slopes, sums):
    member, tile = pl.program_id(0), pl.program_id(1)
    members, tiles = pl.num_programs(0), pl.num_programs(1)
    rows = own.shape[1]
    width = features.shape[2]
    vars_rows = out_weight.shape[0]

    @pl.when((member == 0) & (tile == 0))
    def _():
        sums[...] = jnp.zeros_like(sums)
        grad_ext[...] = jnp.zeros_like(grad_ext)
        for k, part in enumerate((part0, part1, part2, part3)):
            for n in range(2):
                slopes[n, :, pl.ds(pl.multiple_of((me[0] ^ k) * 128, 128), 128)] = part[n]

    here = split(slopes[member, :, pl.ds(pl.multiple_of(tile * points, 128), points)])
    back = dot3(here, split(out_weight[...]), TN)
    sums[2 * width : 2 * width + vars_rows] += dot3(here, split(summed[0]), NN)
    local = edges[...] - (me[1] - 1) * rows
    nodes = lax.broadcasted_iota(jnp.int32, (3 * rows, points), 0)
    scattered = None
    slope_sum = None
    for k in range(4):
        hot = jnp.where(local[k : k + 1] == nodes, 1.0, 0.0).astype(bf16)
        slope_k = slope[0, k]
        slope_sum = slope_k if slope_sum is None else slope_sum + slope_k
        high, low = split(back * slope_k)
        term = jnp.dot(hot, high, preferred_element_type=f32) + jnp.dot(
            hot, low, preferred_element_type=f32
        )
        scattered = term if scattered is None else scattered + term
    grad_ext[member] += scattered
    into_query = back * slope_sum
    grad_query[0] = into_query
    sums[width : 2 * width] += dot3(split(features[0]), split(into_query), TN)

    @pl.when((member == members - 1) & (tile == tiles - 1))
    def _():
        ext = jnp.concatenate([side[n] for n in range(2) for side in (before, own, after)], axis=0)
        grads = jnp.concatenate([grad_ext[0], grad_ext[1]], axis=0)
        sums[0:width] = dot3(split(ext), split(grads), TN)
        for n in range(2):
            for i, side in enumerate((lower, middle, upper)):
                side[n] = grad_ext[n, i * rows : (i + 1) * rows]
        end = 2 * width + vars_rows
        sums[end : end + 8] = jnp.full((8, width), jnp.sum(loss[...]) * (loss_scale / scale), f32)
        for j in range(16):
            for out, core, order in ((keep, me[2], me[3]), (away, 1 - me[2], me[4])):
                at = pl.ds(pl.multiple_of((j ^ order) * 72, 8), 72)
                lanes = pl.ds(pl.multiple_of(core * 256, 128), 256)
                out[j] = sums[at, lanes] * scale


def whole(shape=None):
    return pl.BlockSpec(memory_space=pltpu.VMEM)


def params(dims):
    return pltpu.CompilerParams(dimension_semantics=("arbitrary",) * dims, vmem_limit_bytes=vmem_limit)


def tree(total, parts):
    return (total + parts[0]) + (parts[1] + parts[2])


def placed_at(place, total, parts):
    size = total.shape[0]
    whole_value = jnp.zeros((4 * size,) + total.shape[1:], f32)
    for k, part in enumerate([total] + parts):
        whole_value = lax.dynamic_update_slice(whole_value, part, ((place ^ k) * size, 0, 0))
    return whole_value


def body(mesh_features, grid_features, targets, edges, src_weight, dst_weight, output_weight):
    members, rows, width = mesh_features.shape
    points = grid_features.shape[1]
    count_vars = targets.shape[0]
    var_rows = -(-count_vars // 8) * 8
    slabs = lax.axis_size("grid")
    member, grid = lax.axis_index("member"), lax.axis_index("grid")
    place = place_of(member, grid)
    x_then_y = place["x"] * 4 + place["y"]
    y_then_x = place["y"] * 4 + place["x"]
    straight = place["core"] == 0
    me = jnp.stack([
        member,
        grid,
        place["core"],
        jnp.where(straight, x_then_y, y_then_x),
        jnp.where(straight, y_then_x, x_then_y),
    ]).astype(jnp.int32)

    up = [(i, i + 1) for i in range(slabs - 1)]
    down = [(j, i) for i, j in up]
    before = lax.ppermute(mesh_features, "grid", up)
    after = lax.ppermute(mesh_features, "grid", down)
    query = pl.pallas_call(
        query_kernel,
        grid=(members,),
        in_specs=[pl.BlockSpec((1, points, width), lambda n: (n, 0, 0)), whole()],
        out_specs=pl.BlockSpec((1, points, width), lambda n: (n, 0, 0)),
        out_shape=jax.ShapeDtypeStruct((members, points, width), f32),
        scratch_shapes=[pltpu.VMEM((width, width), bf16)] * 2,
        compiler_params=params(1),
        name="query",
        interpret=interpret,
    )(grid_features, dst_weight)
    edges_t = edges.T
    out_weight = jnp.pad(output_weight.T, ((0, var_rows - count_vars), (0, 0)))
    targets = jnp.pad(targets, ((0, var_rows - count_vars), (0, 0)))

    tile = 512
    part_shape = jax.ShapeDtypeStruct((members, var_rows, 128), f32)
    slope, summed, *parts = pl.pallas_call(
        functools.partial(forward_kernel, tile),
        grid_spec=pltpu.PrefetchScalarGridSpec(
            num_scalar_prefetch=1,
            grid=(members, points // tile),
            in_specs=[
                pl.BlockSpec((1, tile, width), lambda n, t, me: (n, t, 0)),
                pl.BlockSpec((tile, 4), lambda n, t, me: (t, 0)),
                whole(), whole(), whole(), whole(), whole(),
            ],
            out_specs=[
                pl.BlockSpec((1, 4, tile, width), lambda n, t, me: (n, 0, t, 0)),
                pl.BlockSpec((1, tile, width), lambda n, t, me: (n, t, 0)),
            ] + [whole()] * 4,
            scratch_shapes=[
                pltpu.VMEM((members, 256, width), bf16),
                pltpu.VMEM((var_rows, points), f32),
            ],
        ),
        out_shape=[
            jax.ShapeDtypeStruct((members, 4, points, width), f32),
            jax.ShapeDtypeStruct((members, points, width), f32),
        ] + [part_shape] * 4,
        compiler_params=params(2),
        name="forward",
        interpret=interpret,
    )(me, query, edges_t, before, mesh_features, after, src_weight, out_weight)

    to_peer = [[(i, i ^ k) for i in range(4)] for k in range(4)]
    parts = [parts[0]] + [lax.ppermute(parts[k], "member", to_peer[k]) for k in (1, 2, 3)]
    *slopes, loss = pl.pallas_call(
        functools.partial(score_kernel, count_vars),
        grid_spec=pltpu.PrefetchScalarGridSpec(
            num_scalar_prefetch=1,
            grid=(1,),
            in_specs=[whole()] * 4 + [pl.BlockSpec((var_rows, 128), lambda i, me: (0, me[0]))],
            out_specs=[whole()] * 5,
        ),
        out_shape=[part_shape] * 4 + [jax.ShapeDtypeStruct((8, 128), f32)],
        compiler_params=params(1),
        name="score",
        interpret=interpret,
    )(me, *parts, targets)
    slopes = [slopes[0]] + [lax.ppermute(slopes[k], "member", to_peer[k]) for k in (1, 2, 3)]

    total_members = lax.axis_size("member") * members
    scale = 1.0 / (total_members * points * slabs) ** 0.5
    loss_scale = 1.0 / (points * slabs * count_vars)
    chunks = jax.ShapeDtypeStruct((16, 72, 256), f32)
    side = jax.ShapeDtypeStruct((members, rows, width), f32)
    tile = 256
    grad_query, lower, middle, upper, keep, away = pl.pallas_call(
        functools.partial(backward_kernel, tile, scale, loss_scale),
        grid_spec=pltpu.PrefetchScalarGridSpec(
            num_scalar_prefetch=1,
            grid=(members, points // tile),
            in_specs=[whole()] * 5 + [
                pl.BlockSpec((1, 4, tile, width), lambda n, t, me: (n, 0, t, 0)),
                pl.BlockSpec((1, tile, width), lambda n, t, me: (n, t, 0)),
                pl.BlockSpec((1, tile, width), lambda n, t, me: (n, t, 0)),
                pl.BlockSpec((4, tile), lambda n, t, me: (0, t)),
                whole(), whole(), whole(), whole(),
            ],
            out_specs=[
                pl.BlockSpec((1, tile, width), lambda n, t, me: (n, t, 0)),
                whole(), whole(), whole(), whole(), whole(),
            ],
            scratch_shapes=[
                pltpu.VMEM((members, 3 * rows, width), f32),
                pltpu.VMEM((members, var_rows, points), f32),
                pltpu.VMEM((1152, width), f32),
            ],
        ),
        out_shape=[
            jax.ShapeDtypeStruct((members, points, width), f32),
            side,
            side,
            side,
            chunks,
            chunks,
        ],
        compiler_params=params(2),
        name="backward",
        interpret=interpret,
    )(me, *slopes, loss, slope, summed, grid_features, edges, before, mesh_features, after, out_weight)

    core = place["core"]
    first = jnp.where(straight, place["x"], place["y"])
    second = jnp.where(straight, place["y"], place["x"])
    total = keep + send(away, swap_core)
    parts = [send(total[4 * k : 4 * k + 4], first_axis[k]) for k in (1, 2, 3)]
    from_prev = lax.ppermute(upper, "grid", up)
    from_next = lax.ppermute(lower, "grid", down)
    grid_grad = jnp.einsum("npu,wu->npw", grad_query, dst_weight, precision=lax.Precision.HIGH)
    *parts, from_prev, from_next, grid_grad = lax.optimization_barrier(
        (*parts, from_prev, from_next, grid_grad)
    )
    total = tree(total[:4], parts)
    parts = [send(total[k : k + 1], second_axis[k]) for k in (1, 2, 3)]
    mesh_grad = jnp.einsum(
        "nru,wu->nrw", middle + from_prev + from_next, src_weight, precision=lax.Precision.HIGH
    )
    *parts, mesh_grad = lax.optimization_barrier((*parts, mesh_grad))
    total = tree(total[:1], parts)
    total = tree(total, [send(total, along_z[k]) for k in (1, 2, 3)])
    total = total + send(total, along_z[4])
    total = placed_at(second, total, [send(total, second_axis[k]) for k in (1, 2, 3)])
    total = placed_at(first, total, [send(total, first_axis[k]) for k in (1, 2, 3)])
    other = send(total, swap_core).reshape(1152, 256)
    total = total.reshape(1152, 256)
    whole_sum = jnp.where(
        core == 0, jnp.concatenate([total, other], axis=1), jnp.concatenate([other, total], axis=1)
    )
    loss = whole_sum[2 * width + var_rows, 0]
    src_grad = whole_sum[:width]
    dst_grad = whole_sum[width : 2 * width]
    out_grad = whole_sum[2 * width : 2 * width + count_vars].T
    return loss, grid_grad, mesh_grad, src_grad, dst_grad, out_grad


def solution(mesh):
    placed = (
        P("member", "grid", None),
        P("member", "grid", None),
        P(None, "grid"),
        P(None, "grid"),
        P(),
        P(),
        P(),
    )
    return jax.shard_map(
        body,
        mesh=mesh,
        in_specs=placed,
        out_specs=(P(), P("member", "grid", None), P("member", "grid", None), P(), P(), P()),
        check_vma=False,
    )
```

```python
import functools

import jax
import jax.numpy as jnp
from jax import lax
from jax.experimental import pallas as pl
from jax.experimental.pallas import tpu as pltpu
from jax.sharding import PartitionSpec as P

alpha_fair = 0.95
smoothing = 0.1
axes = ("member", "grid")
vmem_limit = 24 * 1024 * 1024
f32 = jnp.float32
bf16 = jnp.bfloat16
interpret = False
node_rows = 32
loss_row = 104


def place_of(member, grid):
    return {
        "core": member & 1,
        "y": ((grid >> 5) << 1) | (member >> 1),
        "z": (grid >> 2) & 7,
        "x": grid & 3,
    }


def exchange(change):
    pairs = []
    for member in range(4):
        for grid in range(64):
            place = place_of(member, grid)
            place = {**place, **change(place)}
            member_to = ((place["y"] & 1) << 1) | place["core"]
            grid_to = ((place["y"] >> 1) << 5) | (place["z"] << 2) | place["x"]
            pairs.append((member * 64 + grid, member_to * 64 + grid_to))
    return pairs


swap_core = exchange(lambda c: {"core": c["core"] ^ 1})
first_axis = [
    exchange(lambda c, k=k: {"x": c["x"] ^ k} if c["core"] == 0 else {"y": c["y"] ^ k}) for k in range(4)
]
second_axis = [
    exchange(lambda c, k=k: {"y": c["y"] ^ k} if c["core"] == 0 else {"x": c["x"] ^ k}) for k in range(4)
]
along_z = [exchange(lambda c, k=k: {"z": c["z"] ^ k}) for k in range(8)]


def send(value, pairs):
    return lax.ppermute(value, axes, pairs)


def split(value):
    high = value.astype(bf16)
    return high, (value - high.astype(f32)).astype(bf16)


def dot3(left, right, dims):
    def one(a, b):
        return lax.dot_general(a, b, (dims, ((), ())), preferred_element_type=f32)

    return one(left[0], right[0]) + (one(left[0], right[1]) + one(left[1], right[0]))


NN = ((1,), (0,))
NT = ((1,), (1,))
TN = ((0,), (0,))


def query_kernel(me, edges, features, weight, src_weight, query, edges_t, src_high, src_low,
                 held, held_weight, held_src, sems):
    members, points = features.shape[0], features.shape[1]
    half = points // 2
    loads = [pltpu.make_async_copy(weight, held_weight, sems.at[0])]
    for i in range(2 * members):
        piece = (i // 2, pl.ds((i % 2) * half, half))
        loads.append(pltpu.make_async_copy(features.at[piece], held.at[piece], sems.at[1 + i]))
    loads.append(pltpu.make_async_copy(src_weight, held_src, sems.at[1 + 2 * members]))
    for load in loads:
        load.start()
    local = edges[...] - (me[1] - 1) * node_rows
    edges_t[...] = jnp.concatenate([local, local], axis=0).T
    loads[0].wait()
    high, low = split(0.5 * held_weight[...])
    for i in range(2 * members):
        loads[1 + i].wait()
        piece = (i // 2, pl.ds((i % 2) * half, half))
        query[piece] = dot3(split(held[piece]), (high, low), NN)
    loads[-1].wait()
    src_high[...], src_low[...] = split(0.5 * held_src[...])


def forward_kernel(points, me, query, edges, before, own, after, src_high, src_low, out_weight,
                   slope, summed, part0, part1, part2, part3, nodes, fields):
    member, tile = pl.program_id(0), pl.program_id(1)
    tiles = pl.num_programs(1)
    rows = own.shape[1]

    @pl.when((member == 0) & (tile == 0))
    def _():
        nodes[...] = jnp.zeros_like(nodes)
        ext = jnp.concatenate([side[n] for n in range(2) for side in (before, own, after)], axis=0)
        high, low = split(dot3(split(ext), (src_high[...], src_low[...]), NN))
        for n in range(2):
            at = slice(n * 3 * rows, (n + 1) * 3 * rows)
            nodes[n, 0 : 3 * rows] = high[at]
            nodes[n, 128 : 128 + 3 * rows] = low[at]

    local = edges[...]
    columns = lax.broadcasted_iota(jnp.int32, (points, 256), 1) & 127
    total = None
    for k in range(4):
        hot = jnp.where(local[:, k : k + 1] == columns, 1.0, 0.0).astype(bf16)
        half = query[0] + jnp.dot(hot, nodes[member], preferred_element_type=f32)
        curve = jnp.tanh(half)
        active = half * curve + half
        curve = 0.5 * curve
        slope[0, k] = (curve + 0.5) + active * (0.5 - curve)
        total = active if total is None else total + active
    summed[0] = total
    weight = split(out_weight[...])
    fields[:, pl.ds(pl.multiple_of(tile * points, 128), points)] = dot3(weight, split(total), NT)

    @pl.when(tile == tiles - 1)
    def _():
        for k, part in enumerate((part0, part1, part2, part3)):
            part[member] = fields[:, pl.ds(pl.multiple_of((me[0] ^ k) * 128, 128), 128)]


def score_kernel(me, part0, part1, part2, part3, targets, out0, out1, out2, out3, loss):
    parts, outs = (part0, part1, part2, part3), (out0, out1, out2, out3)
    count = 8
    spread = (1.0 - alpha_fair) / count
    factor = (1.0 - spread) / (count * (count - 1))
    rows = targets.shape[0]
    near = jnp.zeros((1, 128), f32)
    far = jnp.zeros((1, 128), f32)
    for start in range(0, rows, 8):
        height = min(8, rows - start)
        at = pl.ds(start, height)
        truth = targets[at]
        fields = [parts[j // 2][j % 2, at] for j in range(count)]
        slopes, dist_sum = [], None
        for field in fields:
            error = field - truth
            square = error * error + smoothing * smoothing
            inverse = lax.rsqrt(square)
            dist = square * inverse
            dist_sum = dist if dist_sum is None else dist_sum + dist
            slopes.append(error * inverse * (1.0 / count))
        pair_sum = None
        pairs = [None] * count
        for j in range(count):
            for k in range(j + 1, count):
                differ = fields[j] - fields[k]
                square = differ * differ + smoothing * smoothing
                inverse = lax.rsqrt(square)
                dist = square * inverse - smoothing
                pair_sum = dist if pair_sum is None else pair_sum + dist
                term = differ * inverse
                pairs[j] = term if pairs[j] is None else pairs[j] + term
                pairs[k] = -term if pairs[k] is None else pairs[k] - term
        near += jnp.sum(dist_sum, axis=0, keepdims=True)
        far += jnp.sum(pair_sum, axis=0, keepdims=True)
        for j in range(count):
            outs[j // 2][j % 2, at] = slopes[j] - factor * pairs[j]
    loss[...] = jnp.broadcast_to(near * (1.0 / count) - factor * far, loss.shape)


def backward_kernel(points, scale, loss_scale, me, part0, part1, part2, part3, loss, slope, summed, features,
                    edges, before, own, after, out_weight,
                    grad_query, lower, middle, upper, *rest):
    keep, away, (grad_ext, slopes, sums) = rest[:4], rest[4:8], rest[8:]
    member, tile = pl.program_id(0), pl.program_id(1)
    members, tiles = pl.num_programs(0), pl.num_programs(1)
    rows = own.shape[1]
    width = features.shape[2]
    vars_rows = out_weight.shape[0]

    @pl.when((member == 0) & (tile == 0))
    def _():
        sums[...] = jnp.zeros_like(sums)
        grad_ext[...] = jnp.zeros_like(grad_ext)
        for k, part in enumerate((part0, part1, part2, part3)):
            for n in range(2):
                slopes[n, :, pl.ds(pl.multiple_of((me[0] ^ k) * 128, 128), 128)] = part[n]

    here = split(slopes[member, :, pl.ds(pl.multiple_of(tile * points, 128), points)])
    back = dot3(here, split(out_weight[...]), TN)
    sums[2 * width : 2 * width + vars_rows] += dot3(here, split(summed[0]), NN)
    local = edges[...] - (me[1] - 1) * rows
    nodes = lax.broadcasted_iota(jnp.int32, (3 * rows, points), 0)
    scattered = None
    slope_sum = None
    for k in range(4):
        hot = jnp.where(local[k : k + 1] == nodes, 1.0, 0.0).astype(bf16)
        slope_k = slope[0, k]
        slope_sum = slope_k if slope_sum is None else slope_sum + slope_k
        high, low = split(back * slope_k)
        term = jnp.dot(hot, high, preferred_element_type=f32) + jnp.dot(
            hot, low, preferred_element_type=f32
        )
        scattered = term if scattered is None else scattered + term
    grad_ext[member] += scattered
    into_query = back * slope_sum
    grad_query[0] = into_query
    sums[width : 2 * width] += dot3(split(features[0]), split(into_query), TN)

    @pl.when((member == members - 1) & (tile == tiles - 1))
    def _():
        ext = jnp.concatenate([side[n] for n in range(2) for side in (before, own, after)], axis=0)
        grads = jnp.concatenate([grad_ext[0], grad_ext[1]], axis=0)
        sums[0:width] = dot3(split(ext), split(grads), TN)
        for n in range(2):
            for i, side in enumerate((lower, middle, upper)):
                side[n] = grad_ext[n, i * rows : (i + 1) * rows]
        end = 2 * width + loss_row
        sums[end : end + 8] = jnp.full((8, width), jnp.sum(loss[0:1]) * (loss_scale / scale), f32)
        for j in range(16):
            for out, core, order in ((keep, me[2], me[3]), (away, 1 - me[2], me[4])):
                at = pl.ds(pl.multiple_of((j ^ order) * 72, 8), 72)
                lanes = pl.ds(pl.multiple_of(core * 256, 128), 256)
                out[j // 4][j % 4] = sums[at, lanes] * scale


def whole(shape=None):
    return pl.BlockSpec(memory_space=pltpu.VMEM)


def params(dims):
    return pltpu.CompilerParams(dimension_semantics=("arbitrary",) * dims, vmem_limit_bytes=vmem_limit)


def tree(total, parts):
    return (total + parts[0]) + (parts[1] + parts[2])


def placed_at(place, total, parts):
    size = total.shape[0]
    whole_value = jnp.zeros((4 * size,) + total.shape[1:], f32)
    for k, part in enumerate([total] + parts):
        whole_value = lax.dynamic_update_slice(whole_value, part, ((place ^ k) * size, 0, 0))
    return whole_value


def body(mesh_features, grid_features, targets, edges, src_weight, dst_weight, output_weight):
    members, rows, width = mesh_features.shape
    points = grid_features.shape[1]
    count_vars = targets.shape[0]
    slabs = lax.axis_size("grid")
    member, grid = lax.axis_index("member"), lax.axis_index("grid")
    place = place_of(member, grid)
    x_then_y = place["x"] * 4 + place["y"]
    y_then_x = place["y"] * 4 + place["x"]
    straight = place["core"] == 0
    me = jnp.stack([
        member,
        grid,
        place["core"],
        jnp.where(straight, x_then_y, y_then_x),
        jnp.where(straight, y_then_x, x_then_y),
    ]).astype(jnp.int32)

    up = [(i, i + 1) for i in range(slabs - 1)]
    down = [(j, i) for i, j in up]
    before = lax.ppermute(mesh_features, "grid", up)
    after = lax.ppermute(mesh_features, "grid", down)
    out_weight = output_weight.T
    me_spec = pl.BlockSpec(memory_space=pltpu.SMEM)
    in_hbm = pl.BlockSpec(memory_space=pltpu.HBM)
    query, edges_t, src_high, src_low = pl.pallas_call(
        query_kernel,
        in_specs=[me_spec, whole(), in_hbm, in_hbm, in_hbm],
        out_specs=[whole()] * 4,
        out_shape=[
            jax.ShapeDtypeStruct((members, points, width), f32),
            jax.ShapeDtypeStruct((points, 8), jnp.int32),
            jax.ShapeDtypeStruct((width, width), bf16),
            jax.ShapeDtypeStruct((width, width), bf16),
        ],
        scratch_shapes=[
            pltpu.VMEM((members, points, width), f32),
            pltpu.VMEM((width, width), f32),
            pltpu.VMEM((width, width), f32),
            pltpu.SemaphoreType.DMA((2 + 2 * members,)),
        ],
        compiler_params=pltpu.CompilerParams(vmem_limit_bytes=vmem_limit),
        name="query",
        interpret=interpret,
    )(
        me,
        pltpu.with_memory_space_constraint(edges, pltpu.HBM),
        pltpu.with_memory_space_constraint(grid_features, pltpu.HBM),
        pltpu.with_memory_space_constraint(dst_weight, pltpu.HBM),
        pltpu.with_memory_space_constraint(src_weight, pltpu.HBM),
    )

    tile = 512
    part_shape = jax.ShapeDtypeStruct((members, count_vars, 128), f32)
    slope, summed, *parts = pl.pallas_call(
        functools.partial(forward_kernel, tile),
        grid_spec=pltpu.PrefetchScalarGridSpec(
            num_scalar_prefetch=1,
            grid=(members, points // tile),
            in_specs=[
                pl.BlockSpec((1, tile, width), lambda n, t, me: (n, t, 0)),
                pl.BlockSpec((tile, 8), lambda n, t, me: (t, 0)),
                whole(), whole(), whole(), whole(), whole(), whole(),
            ],
            out_specs=[
                pl.BlockSpec((1, 4, tile, width), lambda n, t, me: (n, 0, t, 0)),
                pl.BlockSpec((1, tile, width), lambda n, t, me: (n, t, 0)),
            ] + [whole()] * 4,
            scratch_shapes=[
                pltpu.VMEM((members, 256, width), bf16),
                pltpu.VMEM((count_vars, points), f32),
            ],
        ),
        out_shape=[
            jax.ShapeDtypeStruct((members, 4, points, width), f32),
            jax.ShapeDtypeStruct((members, points, width), f32),
        ] + [part_shape] * 4,
        compiler_params=params(2),
        name="forward",
        interpret=interpret,
    )(me, query, edges_t, before, mesh_features, after, src_high, src_low, out_weight)

    to_peer = [[(i, i ^ k) for i in range(4)] for k in range(4)]
    parts = [parts[0]] + [lax.ppermute(parts[k], "member", to_peer[k]) for k in (1, 2, 3)]
    *slopes, loss = pl.pallas_call(
        score_kernel,
        grid_spec=pltpu.PrefetchScalarGridSpec(
            num_scalar_prefetch=1,
            grid=(1,),
            in_specs=[whole()] * 4 + [pl.BlockSpec((count_vars, 128), lambda i, me: (0, me[0]))],
            out_specs=[whole()] * 5,
        ),
        out_shape=[part_shape] * 4 + [jax.ShapeDtypeStruct((8, 128), f32)],
        compiler_params=params(1),
        name="score",
        interpret=interpret,
    )(me, *parts, targets)
    slopes = [slopes[0]] + [lax.ppermute(slopes[k], "member", to_peer[k]) for k in (1, 2, 3)]

    total_members = lax.axis_size("member") * members
    scale = 1.0 / (total_members * points * slabs) ** 0.5
    loss_scale = 1.0 / (points * slabs * count_vars)
    chunks = jax.ShapeDtypeStruct((4, 72, 256), f32)
    side = jax.ShapeDtypeStruct((members, rows, width), f32)
    tile = 256
    grad_query, lower, middle, upper, *parts = pl.pallas_call(
        functools.partial(backward_kernel, tile, scale, loss_scale),
        grid_spec=pltpu.PrefetchScalarGridSpec(
            num_scalar_prefetch=1,
            grid=(members, points // tile),
            in_specs=[whole()] * 5 + [
                pl.BlockSpec((1, 4, tile, width), lambda n, t, me: (n, 0, t, 0)),
                pl.BlockSpec((1, tile, width), lambda n, t, me: (n, t, 0)),
                pl.BlockSpec((1, tile, width), lambda n, t, me: (n, t, 0)),
                pl.BlockSpec((4, tile), lambda n, t, me: (0, t)),
                whole(), whole(), whole(), whole(),
            ],
            out_specs=[
                pl.BlockSpec((1, tile, width), lambda n, t, me: (n, t, 0)),
                whole(), whole(), whole(),
            ] + [whole()] * 8,
            scratch_shapes=[
                pltpu.VMEM((members, 3 * rows, width), f32),
                pltpu.VMEM((members, count_vars, points), f32),
                pltpu.VMEM((1152, width), f32),
            ],
        ),
        out_shape=[
            jax.ShapeDtypeStruct((members, points, width), f32),
            side,
            side,
            side,
        ] + [chunks] * 8,
        compiler_params=params(2),
        name="backward",
        interpret=interpret,
    )(me, *slopes, loss, slope, summed, grid_features, edges, before, mesh_features, after, out_weight)

    keep, away = parts[:4], parts[4:]
    core = place["core"]
    first = jnp.where(straight, place["x"], place["y"])
    second = jnp.where(straight, place["y"], place["x"])
    halves = [keep[k] + send(away[k], swap_core) for k in (1, 2, 3, 0)]
    parts = [send(half, first_axis[k]) for k, half in zip((1, 2, 3), halves)]
    grid_grad = jnp.einsum("npu,wu->npw", grad_query, dst_weight, precision=lax.Precision.HIGH)
    upper, lower, grid_grad = lax.optimization_barrier((upper, lower, grid_grad))
    from_prev = lax.ppermute(upper, "grid", up)
    from_next = lax.ppermute(lower, "grid", down)
    *parts, grid_grad = lax.optimization_barrier((*parts, grid_grad))
    total = tree(halves[3], parts)
    parts = [send(total[k : k + 1], second_axis[k]) for k in (1, 2, 3)]
    *parts, from_prev, from_next = lax.optimization_barrier((*parts, from_prev, from_next))
    total = tree(total[:1], parts)
    parts = [send(total, along_z[k]) for k in (1, 2, 3)]
    mesh_grad = jnp.einsum(
        "nru,wu->nrw", middle + from_prev + from_next, src_weight, precision=lax.Precision.HIGH
    )
    *parts, mesh_grad = lax.optimization_barrier((*parts, mesh_grad))
    total = tree(total, parts)
    total = total + send(total, along_z[4])
    total = placed_at(second, total, [send(total, second_axis[k]) for k in (1, 2, 3)])
    parts = [total] + [send(total, first_axis[k]) for k in (1, 2, 3)]
    others = [send(part, swap_core) for part in parts]
    total = placed_at(first, parts[0], parts[1:]).reshape(1152, 256)
    other = placed_at(second, others[0], others[1:]).reshape(1152, 256)
    whole_sum = jnp.where(
        core == 0, jnp.concatenate([total, other], axis=1), jnp.concatenate([other, total], axis=1)
    )
    loss = whole_sum[2 * width + loss_row, 0]
    src_grad = whole_sum[:width]
    dst_grad = whole_sum[width : 2 * width]
    out_grad = whole_sum[2 * width : 2 * width + count_vars].T
    return loss, grid_grad, mesh_grad, src_grad, dst_grad, out_grad


def solution(mesh):
    placed = (
        P("member", "grid", None),
        P("member", "grid", None),
        P(None, "grid"),
        P(None, "grid"),
        P(),
        P(),
        P(),
    )
    return jax.shard_map(
        body,
        mesh=mesh,
        in_specs=placed,
        out_specs=(P(), P("member", "grid", None), P("member", "grid", None), P(), P(), P()),
        check_vma=False,
    )
```

```python
import functools

import jax
import jax.numpy as jnp
from jax import lax
from jax.experimental import pallas as pl
from jax.experimental.pallas import tpu as pltpu
from jax.sharding import PartitionSpec as P

alpha_fair = 0.95
smoothing = 0.1
axes = ("member", "grid")
vmem_limit = 24 * 1024 * 1024
f32 = jnp.float32
bf16 = jnp.bfloat16
interpret = False
node_rows = 32
loss_row = 104


def place_of(member, grid):
    return {
        "core": member & 1,
        "y": ((grid >> 5) << 1) | (member >> 1),
        "z": (grid >> 2) & 7,
        "x": grid & 3,
    }


def exchange(change):
    pairs = []
    for member in range(4):
        for grid in range(64):
            place = place_of(member, grid)
            place = {**place, **change(place)}
            member_to = ((place["y"] & 1) << 1) | place["core"]
            grid_to = ((place["y"] >> 1) << 5) | (place["z"] << 2) | place["x"]
            pairs.append((member * 64 + grid, member_to * 64 + grid_to))
    return pairs


swap_core = exchange(lambda c: {"core": c["core"] ^ 1})
first_axis = [
    exchange(lambda c, k=k: {"x": c["x"] ^ k} if c["core"] == 0 else {"y": c["y"] ^ k}) for k in range(4)
]
second_axis = [
    exchange(lambda c, k=k: {"y": c["y"] ^ k} if c["core"] == 0 else {"x": c["x"] ^ k}) for k in range(4)
]


def shift_z(step):
    return exchange(lambda c: {"z": (c["z"] + step) % 8})


def send(value, pairs):
    return lax.ppermute(value, axes, pairs)


def split(value):
    high = value.astype(bf16)
    return high, (value - high.astype(f32)).astype(bf16)


def dot3(left, right, dims):
    def one(a, b):
        return lax.dot_general(a, b, (dims, ((), ())), preferred_element_type=f32)

    return one(left[0], right[0]) + (one(left[0], right[1]) + one(left[1], right[0]))


NN = ((1,), (0,))
NT = ((1,), (1,))
TN = ((0,), (0,))


def query_kernel(me, edges, features, weight, src_weight, query, edges_t, src_high, src_low,
                 held, held_weight, held_src, sems):
    members, points = features.shape[0], features.shape[1]
    half = points // 2
    loads = [pltpu.make_async_copy(weight, held_weight, sems.at[0])]
    for i in range(2 * members):
        piece = (i // 2, pl.ds((i % 2) * half, half))
        loads.append(pltpu.make_async_copy(features.at[piece], held.at[piece], sems.at[1 + i]))
    loads.append(pltpu.make_async_copy(src_weight, held_src, sems.at[1 + 2 * members]))
    for load in loads:
        load.start()
    local = edges[...] - (me[1] - 1) * node_rows
    edges_t[...] = jnp.concatenate([local, local], axis=0).T
    loads[0].wait()
    high, low = split(0.5 * held_weight[...])
    for i in range(2 * members):
        loads[1 + i].wait()
        piece = (i // 2, pl.ds((i % 2) * half, half))
        query[piece] = dot3(split(held[piece]), (high, low), NN)
    loads[-1].wait()
    src_high[...], src_low[...] = split(0.5 * held_src[...])


def forward_kernel(points, me, query, edges, before, own, after, src_high, src_low, out_weight,
                   slope, summed, part0, part1, part2, part3, nodes, fields):
    member, tile = pl.program_id(0), pl.program_id(1)
    tiles = pl.num_programs(1)
    rows = own.shape[1]

    @pl.when((member == 0) & (tile == 0))
    def _():
        nodes[...] = jnp.zeros_like(nodes)
        ext = jnp.concatenate([side[n] for n in range(2) for side in (before, own, after)], axis=0)
        high, low = split(dot3(split(ext), (src_high[...], src_low[...]), NN))
        for n in range(2):
            at = slice(n * 3 * rows, (n + 1) * 3 * rows)
            nodes[n, 0 : 3 * rows] = high[at]
            nodes[n, 128 : 128 + 3 * rows] = low[at]

    local = edges[...]
    columns = lax.broadcasted_iota(jnp.int32, (points, 256), 1) & 127
    total = None
    for k in range(4):
        hot = jnp.where(local[:, k : k + 1] == columns, 1.0, 0.0).astype(bf16)
        half = query[0] + jnp.dot(hot, nodes[member], preferred_element_type=f32)
        curve = jnp.tanh(half)
        active = half * curve + half
        curve = 0.5 * curve
        slope[0, k] = (curve + 0.5) + active * (0.5 - curve)
        total = active if total is None else total + active
    summed[0] = total
    weight = split(out_weight[...])
    fields[:, pl.ds(pl.multiple_of(tile * points, 128), points)] = dot3(weight, split(total), NT)

    @pl.when(tile == tiles - 1)
    def _():
        for k, part in enumerate((part0, part1, part2, part3)):
            part[member] = fields[:, pl.ds(pl.multiple_of((me[0] ^ k) * 128, 128), 128)]


def score_kernel(me, part0, part1, part2, part3, targets, out0, out1, out2, out3, loss):
    parts, outs = (part0, part1, part2, part3), (out0, out1, out2, out3)
    count = 8
    spread = (1.0 - alpha_fair) / count
    factor = (1.0 - spread) / (count * (count - 1))
    rows = targets.shape[0]
    near = jnp.zeros((1, 128), f32)
    far = jnp.zeros((1, 128), f32)
    for start in range(0, rows, 8):
        height = min(8, rows - start)
        at = pl.ds(start, height)
        truth = targets[at]
        fields = [parts[j // 2][j % 2, at] for j in range(count)]
        slopes, dist_sum = [], None
        for field in fields:
            error = field - truth
            square = error * error + smoothing * smoothing
            inverse = lax.rsqrt(square)
            dist = square * inverse
            dist_sum = dist if dist_sum is None else dist_sum + dist
            slopes.append(error * inverse * (1.0 / count))
        pair_sum = None
        pairs = [None] * count
        for j in range(count):
            for k in range(j + 1, count):
                differ = fields[j] - fields[k]
                square = differ * differ + smoothing * smoothing
                inverse = lax.rsqrt(square)
                dist = square * inverse - smoothing
                pair_sum = dist if pair_sum is None else pair_sum + dist
                term = differ * inverse
                pairs[j] = term if pairs[j] is None else pairs[j] + term
                pairs[k] = -term if pairs[k] is None else pairs[k] - term
        near += jnp.sum(dist_sum, axis=0, keepdims=True)
        far += jnp.sum(pair_sum, axis=0, keepdims=True)
        for j in range(count):
            outs[j // 2][j % 2, at] = slopes[j] - factor * pairs[j]
    loss[...] = jnp.broadcast_to(near * (1.0 / count) - factor * far, loss.shape)


def backward_kernel(points, scale, loss_scale, me, part0, part1, part2, part3, loss, slope, summed, features,
                    edges, before, own, after, out_weight,
                    grad_query, lower, middle, upper, *rest):
    keep, away, (grad_ext, slopes, sums) = rest[:4], rest[4:8], rest[8:]
    member, tile = pl.program_id(0), pl.program_id(1)
    members, tiles = pl.num_programs(0), pl.num_programs(1)
    rows = own.shape[1]
    width = features.shape[2]
    vars_rows = out_weight.shape[0]

    @pl.when((member == 0) & (tile == 0))
    def _():
        sums[...] = jnp.zeros_like(sums)
        grad_ext[...] = jnp.zeros_like(grad_ext)
        for k, part in enumerate((part0, part1, part2, part3)):
            for n in range(2):
                slopes[n, :, pl.ds(pl.multiple_of((me[0] ^ k) * 128, 128), 128)] = part[n]

    here = split(slopes[member, :, pl.ds(pl.multiple_of(tile * points, 128), points)])
    back = dot3(here, split(out_weight[...]), TN)
    sums[2 * width : 2 * width + vars_rows] += dot3(here, split(summed[0]), NN)
    local = edges[...] - (me[1] - 1) * rows
    nodes = lax.broadcasted_iota(jnp.int32, (3 * rows, points), 0)
    scattered = None
    slope_sum = None
    for k in range(4):
        hot = jnp.where(local[k : k + 1] == nodes, 1.0, 0.0).astype(bf16)
        slope_k = slope[0, k]
        slope_sum = slope_k if slope_sum is None else slope_sum + slope_k
        high, low = split(back * slope_k)
        term = jnp.dot(hot, high, preferred_element_type=f32) + jnp.dot(
            hot, low, preferred_element_type=f32
        )
        scattered = term if scattered is None else scattered + term
    grad_ext[member] += scattered
    into_query = back * slope_sum
    grad_query[0] = into_query
    sums[width : 2 * width] += dot3(split(features[0]), split(into_query), TN)

    @pl.when((member == members - 1) & (tile == tiles - 1))
    def _():
        ext = jnp.concatenate([side[n] for n in range(2) for side in (before, own, after)], axis=0)
        grads = jnp.concatenate([grad_ext[0], grad_ext[1]], axis=0)
        sums[0:width] = dot3(split(ext), split(grads), TN)
        for n in range(2):
            for i, side in enumerate((lower, middle, upper)):
                side[n] = grad_ext[n, i * rows : (i + 1) * rows]
        end = 2 * width + loss_row
        sums[end : end + 8] = jnp.full((8, width), jnp.sum(loss[0:1]) * (loss_scale / scale), f32)
        for j in range(16):
            for out, core, order in ((keep, me[2], me[3]), (away, 1 - me[2], me[4])):
                at = pl.ds(pl.multiple_of((j ^ order) * 72, 8), 72)
                lanes = pl.ds(pl.multiple_of(core * 256, 128), 256)
                out[j // 4][j % 4] = sums[at, lanes] * scale


def whole(shape=None):
    return pl.BlockSpec(memory_space=pltpu.VMEM)


def params(dims):
    return pltpu.CompilerParams(dimension_semantics=("arbitrary",) * dims, vmem_limit_bytes=vmem_limit)


def tree(total, parts):
    return (total + parts[0]) + (parts[1] + parts[2])


def placed_at(place, total, parts):
    size = total.shape[0]
    whole_value = jnp.zeros((4 * size,) + total.shape[1:], f32)
    for k, part in enumerate([total] + parts):
        whole_value = lax.dynamic_update_slice(whole_value, part, ((place ^ k) * size, 0, 0))
    return whole_value


def body(mesh_features, grid_features, targets, edges, src_weight, dst_weight, output_weight):
    members, rows, width = mesh_features.shape
    points = grid_features.shape[1]
    count_vars = targets.shape[0]
    slabs = lax.axis_size("grid")
    member, grid = lax.axis_index("member"), lax.axis_index("grid")
    place = place_of(member, grid)
    x_then_y = place["x"] * 4 + place["y"]
    y_then_x = place["y"] * 4 + place["x"]
    straight = place["core"] == 0
    me = jnp.stack([
        member,
        grid,
        place["core"],
        jnp.where(straight, x_then_y, y_then_x),
        jnp.where(straight, y_then_x, x_then_y),
    ]).astype(jnp.int32)

    up = [(i, i + 1) for i in range(slabs - 1)]
    down = [(j, i) for i, j in up]
    before = lax.ppermute(mesh_features, "grid", up)
    after = lax.ppermute(mesh_features, "grid", down)
    out_weight = output_weight.T
    me_spec = pl.BlockSpec(memory_space=pltpu.SMEM)
    in_hbm = pl.BlockSpec(memory_space=pltpu.HBM)
    query, edges_t, src_high, src_low = pl.pallas_call(
        query_kernel,
        in_specs=[me_spec, whole(), in_hbm, in_hbm, in_hbm],
        out_specs=[whole()] * 4,
        out_shape=[
            jax.ShapeDtypeStruct((members, points, width), f32),
            jax.ShapeDtypeStruct((points, 8), jnp.int32),
            jax.ShapeDtypeStruct((width, width), bf16),
            jax.ShapeDtypeStruct((width, width), bf16),
        ],
        scratch_shapes=[
            pltpu.VMEM((members, points, width), f32),
            pltpu.VMEM((width, width), f32),
            pltpu.VMEM((width, width), f32),
            pltpu.SemaphoreType.DMA((2 + 2 * members,)),
        ],
        compiler_params=pltpu.CompilerParams(vmem_limit_bytes=vmem_limit),
        name="query",
        interpret=interpret,
    )(
        me,
        pltpu.with_memory_space_constraint(edges, pltpu.HBM),
        pltpu.with_memory_space_constraint(grid_features, pltpu.HBM),
        pltpu.with_memory_space_constraint(dst_weight, pltpu.HBM),
        pltpu.with_memory_space_constraint(src_weight, pltpu.HBM),
    )

    tile = 512
    part_shape = jax.ShapeDtypeStruct((members, count_vars, 128), f32)
    slope, summed, *parts = pl.pallas_call(
        functools.partial(forward_kernel, tile),
        grid_spec=pltpu.PrefetchScalarGridSpec(
            num_scalar_prefetch=1,
            grid=(members, points // tile),
            in_specs=[
                pl.BlockSpec((1, tile, width), lambda n, t, me: (n, t, 0)),
                pl.BlockSpec((tile, 8), lambda n, t, me: (t, 0)),
                whole(), whole(), whole(), whole(), whole(), whole(),
            ],
            out_specs=[
                pl.BlockSpec((1, 4, tile, width), lambda n, t, me: (n, 0, t, 0)),
                pl.BlockSpec((1, tile, width), lambda n, t, me: (n, t, 0)),
            ] + [whole()] * 4,
            scratch_shapes=[
                pltpu.VMEM((members, 256, width), bf16),
                pltpu.VMEM((count_vars, points), f32),
            ],
        ),
        out_shape=[
            jax.ShapeDtypeStruct((members, 4, points, width), f32),
            jax.ShapeDtypeStruct((members, points, width), f32),
        ] + [part_shape] * 4,
        compiler_params=params(2),
        name="forward",
        interpret=interpret,
    )(me, query, edges_t, before, mesh_features, after, src_high, src_low, out_weight)

    to_peer = [[(i, i ^ k) for i in range(4)] for k in range(4)]
    parts = [parts[0]] + [lax.ppermute(parts[k], "member", to_peer[k]) for k in (1, 2, 3)]
    *slopes, loss = pl.pallas_call(
        score_kernel,
        grid_spec=pltpu.PrefetchScalarGridSpec(
            num_scalar_prefetch=1,
            grid=(1,),
            in_specs=[whole()] * 4 + [pl.BlockSpec((count_vars, 128), lambda i, me: (0, me[0]))],
            out_specs=[whole()] * 5,
        ),
        out_shape=[part_shape] * 4 + [jax.ShapeDtypeStruct((8, 128), f32)],
        compiler_params=params(1),
        name="score",
        interpret=interpret,
    )(me, *parts, targets)
    slopes = [slopes[0]] + [lax.ppermute(slopes[k], "member", to_peer[k]) for k in (1, 2, 3)]

    total_members = lax.axis_size("member") * members
    scale = 1.0 / (total_members * points * slabs) ** 0.5
    loss_scale = 1.0 / (points * slabs * count_vars)
    chunks = jax.ShapeDtypeStruct((4, 72, 256), f32)
    side = jax.ShapeDtypeStruct((members, rows, width), f32)
    tile = 256
    grad_query, lower, middle, upper, *parts = pl.pallas_call(
        functools.partial(backward_kernel, tile, scale, loss_scale),
        grid_spec=pltpu.PrefetchScalarGridSpec(
            num_scalar_prefetch=1,
            grid=(members, points // tile),
            in_specs=[whole()] * 5 + [
                pl.BlockSpec((1, 4, tile, width), lambda n, t, me: (n, 0, t, 0)),
                pl.BlockSpec((1, tile, width), lambda n, t, me: (n, t, 0)),
                pl.BlockSpec((1, tile, width), lambda n, t, me: (n, t, 0)),
                pl.BlockSpec((4, tile), lambda n, t, me: (0, t)),
                whole(), whole(), whole(), whole(),
            ],
            out_specs=[
                pl.BlockSpec((1, tile, width), lambda n, t, me: (n, t, 0)),
                whole(), whole(), whole(),
            ] + [whole()] * 8,
            scratch_shapes=[
                pltpu.VMEM((members, 3 * rows, width), f32),
                pltpu.VMEM((members, count_vars, points), f32),
                pltpu.VMEM((1152, width), f32),
            ],
        ),
        out_shape=[
            jax.ShapeDtypeStruct((members, points, width), f32),
            side,
            side,
            side,
        ] + [chunks] * 8,
        compiler_params=params(2),
        name="backward",
        interpret=interpret,
    )(me, *slopes, loss, slope, summed, grid_features, edges, before, mesh_features, after, out_weight)

    keep, away = parts[:4], parts[4:]
    core = place["core"]
    first = jnp.where(straight, place["x"], place["y"])
    second = jnp.where(straight, place["y"], place["x"])
    swapped = [send(away[k], swap_core) for k in (1, 2, 3, 0)]
    halves = [keep[k] + part for k, part in zip((1, 2, 3), swapped)]
    parts = [send(half, first_axis[k]) for k, half in zip((1, 2, 3), halves)]
    upper, lower, last = lax.optimization_barrier((upper, lower, swapped[3]))
    from_prev = lax.ppermute(upper, "grid", up)
    from_next = lax.ppermute(lower, "grid", down)
    *parts, from_prev, from_next = lax.optimization_barrier((*parts, from_prev, from_next))
    total = tree(keep[0] + last, parts)
    parts = [send(total[k : k + 1], second_axis[k]) for k in (1, 2, 3)]
    mesh_grad = jnp.einsum(
        "nru,wu->nrw", middle + from_prev + from_next, src_weight, precision=lax.Precision.HIGH
    )
    *parts, mesh_grad = lax.optimization_barrier((*parts, mesh_grad))
    total = tree(total[:1], parts)
    above, below = send(total, shift_z(-1)), send(total, shift_z(1))
    pair = total + above
    three = pair + below
    total = three + (send(three, shift_z(-3)) + send(pair, shift_z(3)))
    total = placed_at(second, total, [send(total, second_axis[k]) for k in (1, 2, 3)])
    parts = [total] + [send(total, first_axis[k]) for k in (1, 2, 3)]
    grid_grad = jnp.einsum("npu,wu->npw", grad_query, dst_weight, precision=lax.Precision.HIGH)
    parts[3], grid_grad = lax.optimization_barrier((parts[3], grid_grad))
    others = [send(part, swap_core) for part in parts]
    total = placed_at(first, parts[0], parts[1:]).reshape(1152, 256)
    other = placed_at(second, others[0], others[1:]).reshape(1152, 256)
    whole_sum = jnp.where(
        core == 0, jnp.concatenate([total, other], axis=1), jnp.concatenate([other, total], axis=1)
    )
    loss = whole_sum[2 * width + loss_row, 0]
    src_grad = whole_sum[:width]
    dst_grad = whole_sum[width : 2 * width]
    out_grad = whole_sum[2 * width : 2 * width + count_vars].T
    return loss, grid_grad, mesh_grad, src_grad, dst_grad, out_grad


def solution(mesh):
    placed = (
        P("member", "grid", None),
        P("member", "grid", None),
        P(None, "grid"),
        P(None, "grid"),
        P(),
        P(),
        P(),
    )
    return jax.shard_map(
        body,
        mesh=mesh,
        in_specs=placed,
        out_specs=(P(), P("member", "grid", None), P("member", "grid", None), P(), P(), P()),
        check_vma=False,
    )
```

```python
import functools

import jax
import jax.numpy as jnp
from jax import lax
from jax.experimental import pallas as pl
from jax.experimental.pallas import tpu as pltpu
from jax.sharding import PartitionSpec as P

alpha_fair = 0.95
smoothing = 0.1
axes = ("member", "grid")
vmem_limit = 24 * 1024 * 1024
f32 = jnp.float32
bf16 = jnp.bfloat16
interpret = False
node_rows = 32
loss_row = 104


def place_of(member, grid):
    return {
        "core": member & 1,
        "y": ((grid >> 5) << 1) | (member >> 1),
        "z": (grid >> 2) & 7,
        "x": grid & 3,
    }


def exchange(change):
    pairs = []
    for member in range(4):
        for grid in range(64):
            place = place_of(member, grid)
            place = {**place, **change(place)}
            member_to = ((place["y"] & 1) << 1) | place["core"]
            grid_to = ((place["y"] >> 1) << 5) | (place["z"] << 2) | place["x"]
            pairs.append((member * 64 + grid, member_to * 64 + grid_to))
    return pairs


swap_core = exchange(lambda c: {"core": c["core"] ^ 1})
first_axis = [
    exchange(lambda c, k=k: {"x": c["x"] ^ k} if c["core"] == 0 else {"y": c["y"] ^ k}) for k in range(4)
]
second_axis = [
    exchange(lambda c, k=k: {"y": c["y"] ^ k} if c["core"] == 0 else {"x": c["x"] ^ k}) for k in range(4)
]
along_z = [exchange(lambda c, k=k: {"z": c["z"] ^ k}) for k in range(8)]


def send(value, pairs):
    return lax.ppermute(value, axes, pairs)


def split(value):
    high = value.astype(bf16)
    return high, (value - high.astype(f32)).astype(bf16)


def dot3(left, right, dims):
    def one(a, b):
        return lax.dot_general(a, b, (dims, ((), ())), preferred_element_type=f32)

    return one(left[0], right[0]) + (one(left[0], right[1]) + one(left[1], right[0]))


NN = ((1,), (0,))
NT = ((1,), (1,))
TN = ((0,), (0,))


def query_kernel(me, edges, features, weight, src_weight, query, edges_t, src_high, src_low,
                 held, held_weight, held_src, sems):
    members, points = features.shape[0], features.shape[1]
    half = points // 2
    loads = [pltpu.make_async_copy(weight, held_weight, sems.at[0])]
    for i in range(2 * members):
        piece = (i // 2, pl.ds((i % 2) * half, half))
        loads.append(pltpu.make_async_copy(features.at[piece], held.at[piece], sems.at[1 + i]))
    loads.append(pltpu.make_async_copy(src_weight, held_src, sems.at[1 + 2 * members]))
    for load in loads:
        load.start()
    local = edges[...] - (me[1] - 1) * node_rows
    edges_t[...] = jnp.concatenate([local, local], axis=0).T
    loads[0].wait()
    high, low = split(0.5 * held_weight[...])
    for i in range(2 * members):
        loads[1 + i].wait()
        piece = (i // 2, pl.ds((i % 2) * half, half))
        query[piece] = dot3(split(held[piece]), (high, low), NN)
    loads[-1].wait()
    src_high[...], src_low[...] = split(0.5 * held_src[...])


def forward_kernel(points, me, query, edges, before, own, after, src_high, src_low, out_weight,
                   slope, summed, part0, part1, part2, part3, nodes, fields):
    member, tile = pl.program_id(0), pl.program_id(1)
    tiles = pl.num_programs(1)
    rows = own.shape[1]

    @pl.when((member == 0) & (tile == 0))
    def _():
        nodes[...] = jnp.zeros_like(nodes)
        ext = jnp.concatenate([side[n] for n in range(2) for side in (before, own, after)], axis=0)
        high, low = split(dot3(split(ext), (src_high[...], src_low[...]), NN))
        for n in range(2):
            at = slice(n * 3 * rows, (n + 1) * 3 * rows)
            nodes[n, 0 : 3 * rows] = high[at]
            nodes[n, 128 : 128 + 3 * rows] = low[at]

    local = edges[...]
    columns = lax.broadcasted_iota(jnp.int32, (points, 256), 1) & 127
    total = None
    for k in range(4):
        hot = jnp.where(local[:, k : k + 1] == columns, 1.0, 0.0).astype(bf16)
        half = query[0] + jnp.dot(hot, nodes[member], preferred_element_type=f32)
        curve = jnp.tanh(half)
        active = half * curve + half
        curve = 0.5 * curve
        slope[0, k] = (curve + 0.5) + active * (0.5 - curve)
        total = active if total is None else total + active
    summed[0] = total
    weight = split(out_weight[...])
    fields[:, pl.ds(pl.multiple_of(tile * points, 128), points)] = dot3(weight, split(total), NT)

    @pl.when(tile == tiles - 1)
    def _():
        for k, part in enumerate((part0, part1, part2, part3)):
            part[member] = fields[:, pl.ds(pl.multiple_of((me[0] ^ k) * 128, 128), 128)]


def score_kernel(me, part0, part1, part2, part3, targets, out0, out1, out2, out3, loss):
    parts, outs = (part0, part1, part2, part3), (out0, out1, out2, out3)
    count = 8
    spread = (1.0 - alpha_fair) / count
    factor = (1.0 - spread) / (count * (count - 1))
    rows = targets.shape[0]
    near = jnp.zeros((1, 128), f32)
    far = jnp.zeros((1, 128), f32)
    for start in range(0, rows, 8):
        height = min(8, rows - start)
        at = pl.ds(start, height)
        truth = targets[at]
        fields = [parts[j // 2][j % 2, at] for j in range(count)]
        slopes, dist_sum = [], None
        for field in fields:
            error = field - truth
            square = error * error + smoothing * smoothing
            inverse = lax.rsqrt(square)
            dist = square * inverse
            dist_sum = dist if dist_sum is None else dist_sum + dist
            slopes.append(error * inverse * (1.0 / count))
        pair_sum = None
        pairs = [None] * count
        for j in range(count):
            for k in range(j + 1, count):
                differ = fields[j] - fields[k]
                square = differ * differ + smoothing * smoothing
                inverse = lax.rsqrt(square)
                dist = square * inverse - smoothing
                pair_sum = dist if pair_sum is None else pair_sum + dist
                term = differ * inverse
                pairs[j] = term if pairs[j] is None else pairs[j] + term
                pairs[k] = -term if pairs[k] is None else pairs[k] - term
        near += jnp.sum(dist_sum, axis=0, keepdims=True)
        far += jnp.sum(pair_sum, axis=0, keepdims=True)
        for j in range(count):
            outs[j // 2][j % 2, at] = slopes[j] - factor * pairs[j]
    loss[...] = jnp.broadcast_to(near * (1.0 / count) - factor * far, loss.shape)


def backward_kernel(points, scale, loss_scale, me, part0, part1, part2, part3, loss, slope, summed, features,
                    edges, before, own, after, out_weight,
                    grad_query, lower, middle, upper, *rest):
    keep, away, (grad_ext, slopes, sums) = rest[:4], rest[4:8], rest[8:]
    member, tile = pl.program_id(0), pl.program_id(1)
    members, tiles = pl.num_programs(0), pl.num_programs(1)
    rows = own.shape[1]
    width = features.shape[2]
    vars_rows = out_weight.shape[0]

    @pl.when((member == 0) & (tile == 0))
    def _():
        sums[...] = jnp.zeros_like(sums)
        grad_ext[...] = jnp.zeros_like(grad_ext)
        for k, part in enumerate((part0, part1, part2, part3)):
            for n in range(2):
                slopes[n, :, pl.ds(pl.multiple_of((me[0] ^ k) * 128, 128), 128)] = part[n]

    here = split(slopes[member, :, pl.ds(pl.multiple_of(tile * points, 128), points)])
    back = dot3(here, split(out_weight[...]), TN)
    sums[2 * width : 2 * width + vars_rows] += dot3(here, split(summed[0]), NN)
    local = edges[...] - (me[1] - 1) * rows
    nodes = lax.broadcasted_iota(jnp.int32, (3 * rows, points), 0)
    scattered = None
    slope_sum = None
    for k in range(4):
        hot = jnp.where(local[k : k + 1] == nodes, 1.0, 0.0).astype(bf16)
        slope_k = slope[0, k]
        slope_sum = slope_k if slope_sum is None else slope_sum + slope_k
        high, low = split(back * slope_k)
        term = jnp.dot(hot, high, preferred_element_type=f32) + jnp.dot(
            hot, low, preferred_element_type=f32
        )
        scattered = term if scattered is None else scattered + term
    grad_ext[member] += scattered
    into_query = back * slope_sum
    grad_query[0] = into_query
    sums[width : 2 * width] += dot3(split(features[0]), split(into_query), TN)

    @pl.when((member == members - 1) & (tile == tiles - 1))
    def _():
        ext = jnp.concatenate([side[n] for n in range(2) for side in (before, own, after)], axis=0)
        grads = jnp.concatenate([grad_ext[0], grad_ext[1]], axis=0)
        sums[0:width] = dot3(split(ext), split(grads), TN)
        for n in range(2):
            for i, side in enumerate((lower, middle, upper)):
                side[n] = grad_ext[n, i * rows : (i + 1) * rows]
        end = 2 * width + loss_row
        sums[end : end + 8] = jnp.full((8, width), jnp.sum(loss[0:1]) * (loss_scale / scale), f32)
        for j in range(16):
            for out, core, order in ((keep, me[2], me[3]), (away, 1 - me[2], me[4])):
                at = pl.ds(pl.multiple_of((j ^ order) * 72, 8), 72)
                lanes = pl.ds(pl.multiple_of(core * 256, 128), 256)
                out[j // 4][j % 4] = sums[at, lanes] * scale


def whole(shape=None):
    return pl.BlockSpec(memory_space=pltpu.VMEM)


def params(dims):
    return pltpu.CompilerParams(dimension_semantics=("arbitrary",) * dims, vmem_limit_bytes=vmem_limit)


order = (2, 1, 3)


def tree(total, parts):
    return (total + parts[0]) + (parts[1] + parts[2])


def placed_at(place, total, parts):
    size = total.shape[0]
    whole_value = jnp.zeros((4 * size,) + total.shape[1:], f32)
    for k, part in zip((0,) + order, [total] + parts):
        whole_value = lax.dynamic_update_slice(whole_value, part, ((place ^ k) * size, 0, 0))
    return whole_value


def body(mesh_features, grid_features, targets, edges, src_weight, dst_weight, output_weight):
    members, rows, width = mesh_features.shape
    points = grid_features.shape[1]
    count_vars = targets.shape[0]
    slabs = lax.axis_size("grid")
    member, grid = lax.axis_index("member"), lax.axis_index("grid")
    place = place_of(member, grid)
    x_then_y = place["x"] * 4 + place["y"]
    y_then_x = place["y"] * 4 + place["x"]
    straight = place["core"] == 0
    me = jnp.stack([
        member,
        grid,
        place["core"],
        jnp.where(straight, x_then_y, y_then_x),
        jnp.where(straight, y_then_x, x_then_y),
    ]).astype(jnp.int32)

    up = [(i, i + 1) for i in range(slabs - 1)]
    down = [(j, i) for i, j in up]
    before = lax.ppermute(mesh_features, "grid", up)
    after = lax.ppermute(mesh_features, "grid", down)
    out_weight = output_weight.T
    me_spec = pl.BlockSpec(memory_space=pltpu.SMEM)
    in_hbm = pl.BlockSpec(memory_space=pltpu.HBM)
    query, edges_t, src_high, src_low = pl.pallas_call(
        query_kernel,
        in_specs=[me_spec, whole(), in_hbm, in_hbm, in_hbm],
        out_specs=[whole()] * 4,
        out_shape=[
            jax.ShapeDtypeStruct((members, points, width), f32),
            jax.ShapeDtypeStruct((points, 8), jnp.int32),
            jax.ShapeDtypeStruct((width, width), bf16),
            jax.ShapeDtypeStruct((width, width), bf16),
        ],
        scratch_shapes=[
            pltpu.VMEM((members, points, width), f32),
            pltpu.VMEM((width, width), f32),
            pltpu.VMEM((width, width), f32),
            pltpu.SemaphoreType.DMA((2 + 2 * members,)),
        ],
        compiler_params=pltpu.CompilerParams(vmem_limit_bytes=vmem_limit),
        name="query",
        interpret=interpret,
    )(
        me,
        pltpu.with_memory_space_constraint(edges, pltpu.HBM),
        pltpu.with_memory_space_constraint(grid_features, pltpu.HBM),
        pltpu.with_memory_space_constraint(dst_weight, pltpu.HBM),
        pltpu.with_memory_space_constraint(src_weight, pltpu.HBM),
    )

    tile = 512
    part_shape = jax.ShapeDtypeStruct((members, count_vars, 128), f32)
    slope, summed, *parts = pl.pallas_call(
        functools.partial(forward_kernel, tile),
        grid_spec=pltpu.PrefetchScalarGridSpec(
            num_scalar_prefetch=1,
            grid=(members, points // tile),
            in_specs=[
                pl.BlockSpec((1, tile, width), lambda n, t, me: (n, t, 0)),
                pl.BlockSpec((tile, 8), lambda n, t, me: (t, 0)),
                whole(), whole(), whole(), whole(), whole(), whole(),
            ],
            out_specs=[
                pl.BlockSpec((1, 4, tile, width), lambda n, t, me: (n, 0, t, 0)),
                pl.BlockSpec((1, tile, width), lambda n, t, me: (n, t, 0)),
            ] + [whole()] * 4,
            scratch_shapes=[
                pltpu.VMEM((members, 256, width), bf16),
                pltpu.VMEM((count_vars, points), f32),
            ],
        ),
        out_shape=[
            jax.ShapeDtypeStruct((members, 4, points, width), f32),
            jax.ShapeDtypeStruct((members, points, width), f32),
        ] + [part_shape] * 4,
        compiler_params=params(2),
        name="forward",
        interpret=interpret,
    )(me, query, edges_t, before, mesh_features, after, src_high, src_low, out_weight)

    to_peer = [[(i, i ^ k) for i in range(4)] for k in range(4)]
    parts = [parts[0]] + [lax.ppermute(parts[k], "member", to_peer[k]) for k in (1, 2, 3)]
    *slopes, loss = pl.pallas_call(
        score_kernel,
        grid_spec=pltpu.PrefetchScalarGridSpec(
            num_scalar_prefetch=1,
            grid=(1,),
            in_specs=[whole()] * 4 + [pl.BlockSpec((count_vars, 128), lambda i, me: (0, me[0]))],
            out_specs=[whole()] * 5,
        ),
        out_shape=[part_shape] * 4 + [jax.ShapeDtypeStruct((8, 128), f32)],
        compiler_params=params(1),
        name="score",
        interpret=interpret,
    )(me, *parts, targets)
    slopes = [slopes[0]] + [lax.ppermute(slopes[k], "member", to_peer[k]) for k in (1, 2, 3)]

    total_members = lax.axis_size("member") * members
    scale = 1.0 / (total_members * points * slabs) ** 0.5
    loss_scale = 1.0 / (points * slabs * count_vars)
    chunks = jax.ShapeDtypeStruct((4, 72, 256), f32)
    side = jax.ShapeDtypeStruct((members, rows, width), f32)
    tile = 256
    grad_query, lower, middle, upper, *parts = pl.pallas_call(
        functools.partial(backward_kernel, tile, scale, loss_scale),
        grid_spec=pltpu.PrefetchScalarGridSpec(
            num_scalar_prefetch=1,
            grid=(members, points // tile),
            in_specs=[whole()] * 5 + [
                pl.BlockSpec((1, 4, tile, width), lambda n, t, me: (n, 0, t, 0)),
                pl.BlockSpec((1, tile, width), lambda n, t, me: (n, t, 0)),
                pl.BlockSpec((1, tile, width), lambda n, t, me: (n, t, 0)),
                pl.BlockSpec((4, tile), lambda n, t, me: (0, t)),
                whole(), whole(), whole(), whole(),
            ],
            out_specs=[
                pl.BlockSpec((1, tile, width), lambda n, t, me: (n, t, 0)),
                whole(), whole(), whole(),
            ] + [whole()] * 8,
            scratch_shapes=[
                pltpu.VMEM((members, 3 * rows, width), f32),
                pltpu.VMEM((members, count_vars, points), f32),
                pltpu.VMEM((1152, width), f32),
            ],
        ),
        out_shape=[
            jax.ShapeDtypeStruct((members, points, width), f32),
            side,
            side,
            side,
        ] + [chunks] * 8,
        compiler_params=params(2),
        name="backward",
        interpret=interpret,
    )(me, *slopes, loss, slope, summed, grid_features, edges, before, mesh_features, after, out_weight)

    keep, away = parts[:4], parts[4:]
    core = place["core"]
    first = jnp.where(straight, place["x"], place["y"])
    second = jnp.where(straight, place["y"], place["x"])
    swapped = [send(away[k], swap_core) for k in order + (0,)]
    halves = [keep[k] + part for k, part in zip(order, swapped)]
    parts = [send(half, first_axis[k]) for k, half in zip(order, halves)]
    upper, lower, last = lax.optimization_barrier((upper, lower, swapped[3]))
    from_prev = lax.ppermute(upper, "grid", up)
    from_next = lax.ppermute(lower, "grid", down)
    total = tree(keep[0] + last, parts)
    parts = [send(total[k : k + 1], second_axis[k]) for k in order]
    *parts, from_prev, from_next = lax.optimization_barrier((*parts, from_prev, from_next))
    total = tree(total[:1], parts)
    total = tree(total, [send(total, along_z[k]) for k in order])
    part = send(total, along_z[4])
    grid_grad = jnp.einsum("npu,wu->npw", grad_query, dst_weight, precision=lax.Precision.HIGH)
    mesh_grad = jnp.einsum(
        "nru,wu->nrw", middle + from_prev + from_next, src_weight, precision=lax.Precision.HIGH
    )
    part, grid_grad, mesh_grad = lax.optimization_barrier((part, grid_grad, mesh_grad))
    total = total + part
    total = placed_at(second, total, [send(total, second_axis[k]) for k in order])
    parts = [total] + [send(total, first_axis[k]) for k in order]
    others = [send(part, swap_core) for part in parts]
    total = placed_at(first, parts[0], parts[1:]).reshape(1152, 256)
    other = placed_at(second, others[0], others[1:]).reshape(1152, 256)
    whole_sum = jnp.where(
        core == 0, jnp.concatenate([total, other], axis=1), jnp.concatenate([other, total], axis=1)
    )
    loss = whole_sum[2 * width + loss_row, 0]
    src_grad = whole_sum[:width]
    dst_grad = whole_sum[width : 2 * width]
    out_grad = whole_sum[2 * width : 2 * width + count_vars].T
    return loss, grid_grad, mesh_grad, src_grad, dst_grad, out_grad


def solution(mesh):
    placed = (
        P("member", "grid", None),
        P("member", "grid", None),
        P(None, "grid"),
        P(None, "grid"),
        P(),
        P(),
        P(),
    )
    return jax.shard_map(
        body,
        mesh=mesh,
        in_specs=placed,
        out_specs=(P(), P("member", "grid", None), P("member", "grid", None), P(), P(), P()),
        check_vma=False,
    )
```

```python
import functools

import jax
import jax.numpy as jnp
from jax import lax
from jax.experimental import pallas as pl
from jax.experimental.pallas import tpu as pltpu
from jax.sharding import PartitionSpec as P

alpha_fair = 0.95
smoothing = 0.1
axes = ("member", "grid")
vmem_limit = 24 * 1024 * 1024
f32 = jnp.float32
bf16 = jnp.bfloat16
interpret = False
node_rows = 32
loss_row = 104


def place_of(member, grid):
    return {
        "core": member & 1,
        "y": ((grid >> 5) << 1) | (member >> 1),
        "z": (grid >> 2) & 7,
        "x": grid & 3,
    }


def exchange(change):
    pairs = []
    for member in range(4):
        for grid in range(64):
            place = place_of(member, grid)
            place = {**place, **change(place)}
            member_to = ((place["y"] & 1) << 1) | place["core"]
            grid_to = ((place["y"] >> 1) << 5) | (place["z"] << 2) | place["x"]
            pairs.append((member * 64 + grid, member_to * 64 + grid_to))
    return pairs


swap_core = exchange(lambda c: {"core": c["core"] ^ 1})
first_axis = [
    exchange(lambda c, k=k: {"x": c["x"] ^ k} if c["core"] == 0 else {"y": c["y"] ^ k}) for k in range(4)
]
second_axis = [
    exchange(lambda c, k=k: {"y": c["y"] ^ k} if c["core"] == 0 else {"x": c["x"] ^ k}) for k in range(4)
]
along_z = [exchange(lambda c, k=k: {"z": c["z"] ^ k}) for k in range(8)]


def send(value, pairs):
    return lax.ppermute(value, axes, pairs)


def split(value):
    high = value.astype(bf16)
    return high, (value - high.astype(f32)).astype(bf16)


def dot3(left, right, dims):
    def one(a, b):
        return lax.dot_general(a, b, (dims, ((), ())), preferred_element_type=f32)

    return one(left[0], right[0]) + (one(left[0], right[1]) + one(left[1], right[0]))


NN = ((1,), (0,))
NT = ((1,), (1,))
TN = ((0,), (0,))


def query_kernel(me, edges, features, weight, src_weight, query, edges_t, src_high, src_low,
                 held, held_weight, held_src, sems):
    members, points = features.shape[0], features.shape[1]
    half = points // 2
    loads = [pltpu.make_async_copy(weight, held_weight, sems.at[0])]
    for i in range(2 * members):
        piece = (i // 2, pl.ds((i % 2) * half, half))
        loads.append(pltpu.make_async_copy(features.at[piece], held.at[piece], sems.at[1 + i]))
    loads.append(pltpu.make_async_copy(src_weight, held_src, sems.at[1 + 2 * members]))
    for load in loads:
        load.start()
    local = edges[...] - (me[1] - 1) * node_rows
    edges_t[...] = jnp.concatenate([local, local], axis=0).T
    loads[0].wait()
    high, low = split(0.5 * held_weight[...])
    for i in range(2 * members):
        loads[1 + i].wait()
        piece = (i // 2, pl.ds((i % 2) * half, half))
        query[piece] = dot3(split(held[piece]), (high, low), NN)
    loads[-1].wait()
    src_high[...], src_low[...] = split(0.5 * held_src[...])


def forward(me, member, query, edges, nodes, out_weight, slope, summed, same, flipped):
    points = query.shape[1]
    columns = lax.broadcasted_iota(jnp.int32, (points, 256), 1) & 127
    local = edges[...]
    total = None
    for k in range(4):
        hot = jnp.where(local[:, k : k + 1] == columns, 1.0, 0.0).astype(bf16)
        half = query[0] + jnp.dot(hot, nodes[member], preferred_element_type=f32)
        curve = jnp.tanh(half)
        active = half * curve + half
        curve = 0.5 * curve
        slope[0, k] = (curve + 0.5) + active * (0.5 - curve)
        total = active if total is None else total + active
    summed[0] = total
    fields = dot3(split(out_weight[...]), split(total), NT)
    left, right = fields[:, 0:128], fields[:, 128:256]
    even = (me[0] & 1) == 0
    same[member] = jnp.where(even, left, right)
    flipped[member] = jnp.where(even, right, left)


def far_forward_kernel(me, query, edges, before, own, after, src_high, src_low, out_weight,
                       slope, summed, same, flipped, nodes):
    member = pl.program_id(0)
    rows = own.shape[1]

    @pl.when(member == 0)
    def _():
        nodes[...] = jnp.zeros_like(nodes)
        ext = jnp.concatenate([side[n] for n in range(2) for side in (before, own, after)], axis=0)
        high, low = split(dot3(split(ext), (src_high[...], src_low[...]), NN))
        for n in range(2):
            at = slice(n * 3 * rows, (n + 1) * 3 * rows)
            nodes[n, 0 : 3 * rows] = high[at]
            nodes[n, 128 : 128 + 3 * rows] = low[at]

    forward(me, member, query, edges, nodes, out_weight, slope, summed, same, flipped)


def near_forward_kernel(me, query, edges, nodes, out_weight, slope, summed, same, flipped):
    forward(me, pl.program_id(0), query, edges, nodes, out_weight, slope, summed, same, flipped)


def score_kernel(me, part0, part1, part2, part3, targets, out0, out1, out2, out3, loss):
    parts, outs = (part0, part1, part2, part3), (out0, out1, out2, out3)
    count = 8
    spread = (1.0 - alpha_fair) / count
    factor = (1.0 - spread) / (count * (count - 1))
    rows = targets.shape[0]
    near = jnp.zeros((1, 128), f32)
    far = jnp.zeros((1, 128), f32)
    for start in range(0, rows, 8):
        height = min(8, rows - start)
        at = pl.ds(start, height)
        truth = targets[at]
        fields = [parts[j // 2][j % 2, at] for j in range(count)]
        slopes, dist_sum = [], None
        for field in fields:
            error = field - truth
            square = error * error + smoothing * smoothing
            inverse = lax.rsqrt(square)
            dist = square * inverse
            dist_sum = dist if dist_sum is None else dist_sum + dist
            slopes.append(error * inverse * (1.0 / count))
        pair_sum = None
        pairs = [None] * count
        for j in range(count):
            for k in range(j + 1, count):
                differ = fields[j] - fields[k]
                square = differ * differ + smoothing * smoothing
                inverse = lax.rsqrt(square)
                dist = square * inverse - smoothing
                pair_sum = dist if pair_sum is None else pair_sum + dist
                term = differ * inverse
                pairs[j] = term if pairs[j] is None else pairs[j] + term
                pairs[k] = -term if pairs[k] is None else pairs[k] - term
        near += jnp.sum(dist_sum, axis=0, keepdims=True)
        far += jnp.sum(pair_sum, axis=0, keepdims=True)
        for j in range(count):
            outs[j // 2][j % 2, at] = slopes[j] - factor * pairs[j]
    loss[...] = jnp.broadcast_to(near * (1.0 / count) - factor * far, loss.shape)


def backward(me, member, same, flipped, slope, summed, features, edges, out_weight,
             grad_query, grad_ext, dst_sum, out_sum):
    points = summed.shape[1]
    even = (me[0] & 1) == 0
    one, two = same[member], flipped[member]
    left, right = jnp.where(even, one, two), jnp.where(even, two, one)
    here = split(jnp.concatenate([left, right], axis=1))
    back = dot3(here, split(out_weight[...]), TN)
    out_sum[...] += dot3(here, split(summed[0]), NN)
    local = edges[...] - (me[1] - 1) * node_rows
    nodes = lax.broadcasted_iota(jnp.int32, (3 * node_rows, points), 0)
    scattered = None
    slope_sum = None
    for k in range(4):
        hot = jnp.where(local[k : k + 1] == nodes, 1.0, 0.0).astype(bf16)
        slope_k = slope[0, k]
        slope_sum = slope_k if slope_sum is None else slope_sum + slope_k
        high, low = split(back * slope_k)
        term = jnp.dot(hot, high, preferred_element_type=f32) + jnp.dot(
            hot, low, preferred_element_type=f32
        )
        scattered = term if scattered is None else scattered + term
    grad_ext[member] += scattered
    into_query = back * slope_sum
    grad_query[0] = into_query
    dst_sum[...] += dot3(split(features[0]), split(into_query), TN)


def near_backward_kernel(me, same, flipped, slope, summed, features, edges, out_weight,
                         grad_query, grad_ext, dst_sum, out_sum):
    member = pl.program_id(0)

    @pl.when(member == 0)
    def _():
        for total in (grad_ext, dst_sum, out_sum):
            total[...] = jnp.zeros_like(total)

    backward(me, member, same, flipped, slope, summed, features, edges, out_weight,
             grad_query, grad_ext, dst_sum, out_sum)


def far_backward_kernel(scale, loss_scale, me, same, flipped, slope, summed, features, edges, out_weight,
                        near_ext, near_dst, near_out, loss, before, own, after,
                        grad_query, lower, middle, upper, *rest):
    keep, away, (grad_ext, sums) = rest[:4], rest[4:8], rest[8:]
    member = pl.program_id(0)
    rows = own.shape[1]
    width = features.shape[2]
    count_vars = out_weight.shape[0]
    dst_sum = sums.at[width : 2 * width]
    out_sum = sums.at[2 * width : 2 * width + count_vars]

    @pl.when(member == 0)
    def _():
        sums[2 * width :] = jnp.zeros((sums.shape[0] - 2 * width, width), f32)
        grad_ext[...] = near_ext[...]
        dst_sum[...] = near_dst[...]
        out_sum[...] = near_out[...]

    backward(me, member, same, flipped, slope, summed, features, edges, out_weight,
             grad_query, grad_ext, dst_sum, out_sum)

    @pl.when(member == pl.num_programs(0) - 1)
    def _():
        ext = jnp.concatenate([side[n] for n in range(2) for side in (before, own, after)], axis=0)
        grads = jnp.concatenate([grad_ext[0], grad_ext[1]], axis=0)
        sums[0:width] = dot3(split(ext), split(grads), TN)
        for n in range(2):
            for i, side in enumerate((lower, middle, upper)):
                side[n] = grad_ext[n, i * rows : (i + 1) * rows]
        end = 2 * width + loss_row
        sums[end : end + 8] = jnp.full((8, width), jnp.sum(loss[0:1]) * (loss_scale / scale), f32)
        for j in range(16):
            for out, core, order in ((keep, me[2], me[3]), (away, 1 - me[2], me[4])):
                at = pl.ds(pl.multiple_of((j ^ order) * 72, 8), 72)
                lanes = pl.ds(pl.multiple_of(core * 256, 128), 256)
                out[j // 4][j % 4] = sums[at, lanes] * scale


def whole(shape=None):
    return pl.BlockSpec(memory_space=pltpu.VMEM)


def params(dims):
    return pltpu.CompilerParams(dimension_semantics=("arbitrary",) * dims, vmem_limit_bytes=vmem_limit)


order = (2, 1, 3)


def tree(total, parts):
    return (total + parts[0]) + (parts[1] + parts[2])


def placed_at(place, total, parts):
    size = total.shape[0]
    whole_value = jnp.zeros((4 * size,) + total.shape[1:], f32)
    for k, part in zip((0,) + order, [total] + parts):
        whole_value = lax.dynamic_update_slice(whole_value, part, ((place ^ k) * size, 0, 0))
    return whole_value


def body(mesh_features, grid_features, targets, edges, src_weight, dst_weight, output_weight):
    members, rows, width = mesh_features.shape
    points = grid_features.shape[1]
    count_vars = targets.shape[0]
    slabs = lax.axis_size("grid")
    member, grid = lax.axis_index("member"), lax.axis_index("grid")
    place = place_of(member, grid)
    x_then_y = place["x"] * 4 + place["y"]
    y_then_x = place["y"] * 4 + place["x"]
    straight = place["core"] == 0
    me = jnp.stack([
        member,
        grid,
        place["core"],
        jnp.where(straight, x_then_y, y_then_x),
        jnp.where(straight, y_then_x, x_then_y),
    ]).astype(jnp.int32)

    up = [(i, i + 1) for i in range(slabs - 1)]
    down = [(j, i) for i, j in up]
    before = lax.ppermute(mesh_features, "grid", up)
    after = lax.ppermute(mesh_features, "grid", down)
    out_weight = output_weight.T
    me_spec = pl.BlockSpec(memory_space=pltpu.SMEM)
    in_hbm = pl.BlockSpec(memory_space=pltpu.HBM)
    query, edges_t, src_high, src_low = pl.pallas_call(
        query_kernel,
        in_specs=[me_spec, whole(), in_hbm, in_hbm, in_hbm],
        out_specs=[whole()] * 4,
        out_shape=[
            jax.ShapeDtypeStruct((members, points, width), f32),
            jax.ShapeDtypeStruct((points, 8), jnp.int32),
            jax.ShapeDtypeStruct((width, width), bf16),
            jax.ShapeDtypeStruct((width, width), bf16),
        ],
        scratch_shapes=[
            pltpu.VMEM((members, points, width), f32),
            pltpu.VMEM((width, width), f32),
            pltpu.VMEM((width, width), f32),
            pltpu.SemaphoreType.DMA((2 + 2 * members,)),
        ],
        compiler_params=pltpu.CompilerParams(vmem_limit_bytes=vmem_limit),
        name="query",
        interpret=interpret,
    )(
        me,
        pltpu.with_memory_space_constraint(edges, pltpu.HBM),
        pltpu.with_memory_space_constraint(grid_features, pltpu.HBM),
        pltpu.with_memory_space_constraint(dst_weight, pltpu.HBM),
        pltpu.with_memory_space_constraint(src_weight, pltpu.HBM),
    )

    half = points // 2

    def near(me):
        return me[0] >> 1

    def far(me):
        return 1 - (me[0] >> 1)

    def rows_of(side):
        return pl.BlockSpec((1, half, width), lambda n, me: (n, side(me), 0))

    halves = pl.BlockSpec((1, half, width), lambda n, me: (n, 0, 0))
    half_slopes = pl.BlockSpec((1, 4, half, width), lambda n, me: (n, 0, 0, 0))
    part_shape = jax.ShapeDtypeStruct((members, count_vars, 128), f32)
    half_shape = jax.ShapeDtypeStruct((members, half, width), f32)
    slopes_shape = jax.ShapeDtypeStruct((members, 4, half, width), f32)

    def call(kernel, name, work, in_specs, out_specs, out_shape, scratch=()):
        return pl.pallas_call(
            kernel,
            grid_spec=pltpu.PrefetchScalarGridSpec(
                num_scalar_prefetch=1,
                grid=(members,),
                in_specs=in_specs,
                out_specs=out_specs,
                scratch_shapes=list(scratch),
            ),
            out_shape=out_shape,
            compiler_params=params(1),
            cost_estimate=pl.CostEstimate(
                flops=work, bytes_accessed=4 * members * points * width, transcendentals=0
            ),
            name=name,
            interpret=interpret,
        )

    forward_work = 2 * members * half * width * (4 * 256 + 3 * count_vars + 1024)
    backward_work = 2 * members * half * width * (8 * 256 + 6 * count_vars + 3 * width)
    far_slope, far_summed, part2, part3, nodes = call(
        far_forward_kernel,
        "far_forward",
        forward_work,
        [rows_of(far), pl.BlockSpec((half, 8), lambda n, me: (far(me), 0))] + [whole()] * 6,
        [half_slopes, halves] + [whole()] * 3,
        [slopes_shape, half_shape, part_shape, part_shape]
        + [jax.ShapeDtypeStruct((members, 256, width), bf16)],
    )(me, query, edges_t, before, mesh_features, after, src_high, src_low, out_weight)
    to_peer = [[(i, i ^ k) for i in range(4)] for k in range(4)]
    part2 = lax.ppermute(part2, "member", to_peer[2])
    part3 = lax.ppermute(part3, "member", to_peer[3])
    near_slope, near_summed, part0, part1 = call(
        near_forward_kernel,
        "near_forward",
        forward_work,
        [rows_of(near), pl.BlockSpec((half, 8), lambda n, me: (near(me), 0))] + [whole()] * 2,
        [half_slopes, halves] + [whole()] * 2,
        [slopes_shape, half_shape, part_shape, part_shape],
    )(me, query, edges_t, nodes, out_weight)
    part0, part1, part2, part3 = lax.optimization_barrier((part0, part1, part2, part3))
    part1 = lax.ppermute(part1, "member", to_peer[1])

    *slopes, loss = pl.pallas_call(
        score_kernel,
        grid_spec=pltpu.PrefetchScalarGridSpec(
            num_scalar_prefetch=1,
            grid=(1,),
            in_specs=[whole()] * 4 + [pl.BlockSpec((count_vars, 128), lambda i, me: (0, me[0]))],
            out_specs=[whole()] * 5,
        ),
        out_shape=[part_shape] * 4 + [jax.ShapeDtypeStruct((8, 128), f32)],
        compiler_params=params(1),
        name="score",
        interpret=interpret,
    )(me, part0, part1, part2, part3, targets)

    total_members = lax.axis_size("member") * members
    scale = 1.0 / (total_members * points * slabs) ** 0.5
    loss_scale = 1.0 / (points * slabs * count_vars)
    ext_shape = jax.ShapeDtypeStruct((members, 3 * rows, width), f32)
    out_sum_shape = jax.ShapeDtypeStruct((count_vars, width), f32)
    side = jax.ShapeDtypeStruct((members, rows, width), f32)
    chunks = jax.ShapeDtypeStruct((4, 72, 256), f32)

    def backward_specs(which):
        return [whole()] * 2 + [
            half_slopes,
            halves,
            rows_of(which),
            pl.BlockSpec((4, half), lambda n, me: (0, which(me))),
            whole(),
        ]

    slope1 = lax.ppermute(slopes[1], "member", to_peer[1])
    slope2 = lax.ppermute(slopes[2], "member", to_peer[2])
    slope3 = lax.ppermute(slopes[3], "member", to_peer[3])
    near_grad, near_ext, near_dst, near_out = call(
        near_backward_kernel,
        "near_backward",
        backward_work,
        backward_specs(near),
        [halves] + [whole()] * 3,
        [half_shape, ext_shape, jax.ShapeDtypeStruct((width, width), f32), out_sum_shape],
    )(me, slopes[0], slope1, near_slope, near_summed, grid_features, edges, out_weight)
    slope2, slope3, near_dst = lax.optimization_barrier((slope2, slope3, near_dst))
    far_grad, lower, middle, upper, *parts = call(
        functools.partial(far_backward_kernel, scale, loss_scale),
        "far_backward",
        backward_work,
        backward_specs(far) + [whole()] * 7,
        [halves] + [whole()] * 11,
        [half_shape] + [side] * 3 + [chunks] * 8,
        [pltpu.VMEM((members, 3 * rows, width), f32), pltpu.VMEM((1152, width), f32)],
    )(me, slope2, slope3, far_slope, far_summed, grid_features, edges, out_weight,
      near_ext, near_dst, near_out, loss, before, mesh_features, after)
    grad_query = jnp.where(
        member < 2,
        jnp.concatenate([near_grad, far_grad], axis=1),
        jnp.concatenate([far_grad, near_grad], axis=1),
    )

    keep, away = parts[:4], parts[4:]
    core = place["core"]
    first = jnp.where(straight, place["x"], place["y"])
    second = jnp.where(straight, place["y"], place["x"])
    swapped = [send(away[k], swap_core) for k in order + (0,)]
    halves = [keep[k] + part for k, part in zip(order, swapped)]
    parts = [send(half, first_axis[k]) for k, half in zip(order, halves)]
    upper, lower, last = lax.optimization_barrier((upper, lower, swapped[3]))
    from_prev = lax.ppermute(upper, "grid", up)
    from_next = lax.ppermute(lower, "grid", down)
    total = tree(keep[0] + last, parts)
    parts = [send(total[k : k + 1], second_axis[k]) for k in order]
    *parts, from_prev, from_next = lax.optimization_barrier((*parts, from_prev, from_next))
    total = tree(total[:1], parts)
    total = tree(total, [send(total, along_z[k]) for k in order])
    part = send(total, along_z[4])
    grid_grad = jnp.einsum("npu,wu->npw", grad_query, dst_weight, precision=lax.Precision.HIGH)
    mesh_grad = jnp.einsum(
        "nru,wu->nrw", middle + from_prev + from_next, src_weight, precision=lax.Precision.HIGH
    )
    part, grid_grad, mesh_grad = lax.optimization_barrier((part, grid_grad, mesh_grad))
    total = total + part
    total = placed_at(second, total, [send(total, second_axis[k]) for k in order])
    parts = [total] + [send(total, first_axis[k]) for k in order]
    others = [send(part, swap_core) for part in parts]
    total = placed_at(first, parts[0], parts[1:]).reshape(1152, 256)
    other = placed_at(second, others[0], others[1:]).reshape(1152, 256)
    whole_sum = jnp.where(
        core == 0, jnp.concatenate([total, other], axis=1), jnp.concatenate([other, total], axis=1)
    )
    loss = whole_sum[2 * width + loss_row, 0]
    src_grad = whole_sum[:width]
    dst_grad = whole_sum[width : 2 * width]
    out_grad = whole_sum[2 * width : 2 * width + count_vars].T
    return loss, grid_grad, mesh_grad, src_grad, dst_grad, out_grad


def solution(mesh):
    placed = (
        P("member", "grid", None),
        P("member", "grid", None),
        P(None, "grid"),
        P(None, "grid"),
        P(),
        P(),
        P(),
    )
    return jax.shard_map(
        body,
        mesh=mesh,
        in_specs=placed,
        out_specs=(P(), P("member", "grid", None), P("member", "grid", None), P(), P(), P()),
        check_vma=False,
    )
```

```python
import functools

import jax
import jax.numpy as jnp
from jax import lax
from jax.experimental import pallas as pl
from jax.experimental.pallas import tpu as pltpu
from jax.sharding import PartitionSpec as P

alpha_fair = 0.95
smoothing = 0.1
axes = ("member", "grid")
vmem_limit = 24 * 1024 * 1024
f32 = jnp.float32
bf16 = jnp.bfloat16
interpret = False
node_rows = 32
loss_row = 104


def place_of(member, grid):
    return {
        "core": member & 1,
        "y": ((grid >> 5) << 1) | (member >> 1),
        "z": (grid >> 2) & 7,
        "x": grid & 3,
    }


def exchange(change):
    pairs = []
    for member in range(4):
        for grid in range(64):
            place = place_of(member, grid)
            place = {**place, **change(place)}
            member_to = ((place["y"] & 1) << 1) | place["core"]
            grid_to = ((place["y"] >> 1) << 5) | (place["z"] << 2) | place["x"]
            pairs.append((member * 64 + grid, member_to * 64 + grid_to))
    return pairs


swap_core = exchange(lambda c: {"core": c["core"] ^ 1})
first_axis = [
    exchange(lambda c, k=k: {"x": c["x"] ^ k} if c["core"] == 0 else {"y": c["y"] ^ k}) for k in range(4)
]
second_axis = [
    exchange(lambda c, k=k: {"y": c["y"] ^ k} if c["core"] == 0 else {"x": c["x"] ^ k}) for k in range(4)
]
along_z = [exchange(lambda c, k=k: {"z": c["z"] ^ k}) for k in range(8)]


def send(value, pairs):
    return lax.ppermute(value, axes, pairs)


def split(value):
    high = value.astype(bf16)
    return high, (value - high.astype(f32)).astype(bf16)


def dot3(left, right, dims):
    def one(a, b):
        return lax.dot_general(a, b, (dims, ((), ())), preferred_element_type=f32)

    return one(left[0], right[0]) + (one(left[0], right[1]) + one(left[1], right[0]))


NN = ((1,), (0,))
NT = ((1,), (1,))
TN = ((0,), (0,))


def query_kernel(me, edges, features, weight, src_weight, query, edges_t, src_high, src_low,
                 held, held_weight, held_src, sems):
    members, points = features.shape[0], features.shape[1]
    half = points // 2
    loads = [pltpu.make_async_copy(weight, held_weight, sems.at[0])]
    for i in range(2 * members):
        piece = (i // 2, pl.ds((i % 2) * half, half))
        loads.append(pltpu.make_async_copy(features.at[piece], held.at[piece], sems.at[1 + i]))
    loads.append(pltpu.make_async_copy(src_weight, held_src, sems.at[1 + 2 * members]))
    loads[0].start()
    loads[1].start()
    local = edges[...] - (me[1] - 1) * node_rows
    edges_t[...] = jnp.concatenate([local, local], axis=0).T
    loads[0].wait()
    for load in loads[2:]:
        load.start()
    high, low = split(0.5 * held_weight[...])
    for i in range(2 * members):
        loads[1 + i].wait()
        piece = (i // 2, pl.ds((i % 2) * half, half))
        query[piece] = dot3(split(held[piece]), (high, low), NN)
    loads[-1].wait()
    src_high[...], src_low[...] = split(0.5 * held_src[...])


def chunk_rows(width):
    return ((0, 0, 32), (32, width, 32), (64, 2 * width, 8))


def forward(me, member, query, edges, nodes, out_weight, slope, summed, same, flipped):
    points = query.shape[1]
    columns = lax.broadcasted_iota(jnp.int32, (points, 256), 1) & 127
    local = edges[...]
    total = None
    for k in range(4):
        hot = jnp.where(local[:, k : k + 1] == columns, 1.0, 0.0).astype(bf16)
        half = query[0] + jnp.dot(hot, nodes[member], preferred_element_type=f32)
        curve = jnp.tanh(half)
        active = half * curve + half
        curve = 0.5 * curve
        slope[0, k] = (curve + 0.5) + active * (0.5 - curve)
        total = active if total is None else total + active
    summed[0] = total
    fields = dot3(split(out_weight[...]), split(total), NT)
    left, right = fields[:, 0:128], fields[:, 128:256]
    even = (me[0] & 1) == 0
    same[member] = jnp.where(even, left, right)
    flipped[member] = jnp.where(even, right, left)


def far_forward_kernel(me, query, edges, before, own, after, src_high, src_low, out_weight,
                       slope, summed, same, flipped, nodes):
    member = pl.program_id(0)
    rows = own.shape[1]

    @pl.when(member == 0)
    def _():
        nodes[...] = jnp.zeros_like(nodes)
        ext = jnp.concatenate([side[n] for n in range(2) for side in (before, own, after)], axis=0)
        high, low = split(dot3(split(ext), (src_high[...], src_low[...]), NN))
        for n in range(2):
            at = slice(n * 3 * rows, (n + 1) * 3 * rows)
            nodes[n, 0 : 3 * rows] = high[at]
            nodes[n, 128 : 128 + 3 * rows] = low[at]

    forward(me, member, query, edges, nodes, out_weight, slope, summed, same, flipped)


def near_forward_kernel(me, query, edges, nodes, out_weight, slope, summed, same, flipped):
    forward(me, pl.program_id(0), query, edges, nodes, out_weight, slope, summed, same, flipped)


def score_kernel(me, part0, part1, part2, part3, targets, out0, out1, out2, out3, loss):
    parts, outs = (part0, part1, part2, part3), (out0, out1, out2, out3)
    count = 8
    spread = (1.0 - alpha_fair) / count
    factor = (1.0 - spread) / (count * (count - 1))
    rows = targets.shape[0]
    near = jnp.zeros((1, 128), f32)
    far = jnp.zeros((1, 128), f32)
    for start in range(0, rows, 8):
        height = min(8, rows - start)
        at = pl.ds(start, height)
        truth = targets[at]
        fields = [parts[j // 2][j % 2, at] for j in range(count)]
        slopes, dist_sum = [], None
        for field in fields:
            error = field - truth
            square = error * error + smoothing * smoothing
            inverse = lax.rsqrt(square)
            dist = square * inverse
            dist_sum = dist if dist_sum is None else dist_sum + dist
            slopes.append(error * inverse * (1.0 / count))
        pair_sum = None
        pairs = [None] * count
        for j in range(count):
            for k in range(j + 1, count):
                differ = fields[j] - fields[k]
                square = differ * differ + smoothing * smoothing
                inverse = lax.rsqrt(square)
                dist = square * inverse - smoothing
                pair_sum = dist if pair_sum is None else pair_sum + dist
                term = differ * inverse
                pairs[j] = term if pairs[j] is None else pairs[j] + term
                pairs[k] = -term if pairs[k] is None else pairs[k] - term
        near += jnp.sum(dist_sum, axis=0, keepdims=True)
        far += jnp.sum(pair_sum, axis=0, keepdims=True)
        for j in range(count):
            outs[j // 2][j % 2, at] = slopes[j] - factor * pairs[j]
    loss[...] = jnp.broadcast_to(near * (1.0 / count) - factor * far, loss.shape)


def backward(me, member, same, flipped, slope, summed, features, edges, out_weight,
             grad_query, grad_ext, dst_sum, out_sum):
    points = summed.shape[1]
    even = (me[0] & 1) == 0
    one, two = same[member], flipped[member]
    left, right = jnp.where(even, one, two), jnp.where(even, two, one)
    here = split(jnp.concatenate([left, right], axis=1))
    back = dot3(here, split(out_weight[...]), TN)
    out_sum[...] += dot3(here, split(summed[0]), NN)
    local = edges[...] - (me[1] - 1) * node_rows
    nodes = lax.broadcasted_iota(jnp.int32, (3 * node_rows, points), 0)
    scattered = None
    slope_sum = None
    for k in range(4):
        hot = jnp.where(local[k : k + 1] == nodes, 1.0, 0.0).astype(bf16)
        slope_k = slope[0, k]
        slope_sum = slope_k if slope_sum is None else slope_sum + slope_k
        high, low = split(back * slope_k)
        term = jnp.dot(hot, high, preferred_element_type=f32) + jnp.dot(
            hot, low, preferred_element_type=f32
        )
        scattered = term if scattered is None else scattered + term
    grad_ext[member] += scattered
    into_query = back * slope_sum
    grad_query[0] = into_query
    dst_sum[...] += dot3(split(features[0]), split(into_query), TN)


def near_backward_kernel(me, same, flipped, slope, summed, features, edges, out_weight,
                         grad_query, grad_ext, dst_sum, out_sum):
    member = pl.program_id(0)

    @pl.when(member == 0)
    def _():
        for total in (grad_ext, dst_sum, out_sum):
            total[...] = jnp.zeros_like(total)

    backward(me, member, same, flipped, slope, summed, features, edges, out_weight,
             grad_query, grad_ext, dst_sum, out_sum)


def far_backward_kernel(scale, loss_scale, me, same, flipped, slope, summed, features, edges, out_weight,
                        near_ext, near_dst, near_out, loss, before, own, after,
                        grad_query, lower, middle, upper, *rest):
    keep, away, (grad_ext, sums) = rest[:4], rest[4:8], rest[8:]
    member = pl.program_id(0)
    rows = own.shape[1]
    width = features.shape[2]
    count_vars = out_weight.shape[0]
    dst_sum = sums.at[width : 2 * width]
    out_sum = sums.at[2 * width : 2 * width + count_vars]

    @pl.when(member == 0)
    def _():
        sums[2 * width :] = jnp.zeros((sums.shape[0] - 2 * width, width), f32)
        grad_ext[...] = near_ext[...]
        dst_sum[...] = near_dst[...]
        out_sum[...] = near_out[...]

    backward(me, member, same, flipped, slope, summed, features, edges, out_weight,
             grad_query, grad_ext, dst_sum, out_sum)

    @pl.when(member == pl.num_programs(0) - 1)
    def _():
        ext = jnp.concatenate([side[n] for n in range(2) for side in (before, own, after)], axis=0)
        grads = jnp.concatenate([grad_ext[0], grad_ext[1]], axis=0)
        sums[0:width] = dot3(split(ext), split(grads), TN)
        for n in range(2):
            for i, side in enumerate((lower, middle, upper)):
                side[n] = grad_ext[n, i * rows : (i + 1) * rows]
        end = 2 * width + loss_row
        sums[end : end + 8] = jnp.full((8, width), jnp.sum(loss[0:1]) * (loss_scale / scale), f32)
        for j in range(16):
            for out, core, order in ((keep, me[2], me[3]), (away, 1 - me[2], me[4])):
                chunk = j ^ order
                lanes = pl.ds(pl.multiple_of(core * 256, 128), 256)
                for to, start, height in chunk_rows(width):
                    at = pl.ds(pl.multiple_of(start + chunk * height, 8), height)
                    out[j // 4][j % 4, to : to + height] = sums[at, lanes] * scale


def finish_kernel(me, *refs):
    parts, (src_grad, dst_grad, out_grad, loss, rest) = refs[:8], refs[8:]
    width = src_grad.shape[0]
    for i, part in enumerate(parts):
        core, order = (me[2], me[3]) if i < 4 else (1 - me[2], me[4])
        group = (order >> 2) ^ peer_order[i % 4]
        lanes = pl.ds(pl.multiple_of(core * 256, 128), 256)
        for j in range(4):
            for out, (to, _, height) in zip((src_grad, dst_grad, rest), chunk_rows(width)):
                at = pl.ds(pl.multiple_of((group * 4 + j) * height, 8), height)
                out[at, lanes] = part[j, to : to + height]
    out_grad[...] = rest[0 : out_grad.shape[0]]
    loss[0, 0] = jnp.max(rest[loss_row : loss_row + 8, 0:128])


def whole(shape=None):
    return pl.BlockSpec(memory_space=pltpu.VMEM)


def params(dims):
    return pltpu.CompilerParams(dimension_semantics=("arbitrary",) * dims, vmem_limit_bytes=vmem_limit)


order = (2, 1, 3)
peer_order = (0,) + order


def tree(total, parts):
    return (total + parts[0]) + (parts[1] + parts[2])


def placed_at(place, total, parts):
    size = total.shape[0]
    whole_value = jnp.zeros((4 * size,) + total.shape[1:], f32)
    for k, part in zip((0,) + order, [total] + parts):
        whole_value = lax.dynamic_update_slice(whole_value, part, ((place ^ k) * size, 0, 0))
    return whole_value


def body(mesh_features, grid_features, targets, edges, src_weight, dst_weight, output_weight):
    members, rows, width = mesh_features.shape
    points = grid_features.shape[1]
    count_vars = targets.shape[0]
    slabs = lax.axis_size("grid")
    member, grid = lax.axis_index("member"), lax.axis_index("grid")
    place = place_of(member, grid)
    x_then_y = place["x"] * 4 + place["y"]
    y_then_x = place["y"] * 4 + place["x"]
    straight = place["core"] == 0
    me = jnp.stack([
        member,
        grid,
        place["core"],
        jnp.where(straight, x_then_y, y_then_x),
        jnp.where(straight, y_then_x, x_then_y),
    ]).astype(jnp.int32)

    up = [(i, i + 1) for i in range(slabs - 1)]
    down = [(j, i) for i, j in up]
    before = lax.ppermute(mesh_features, "grid", up)
    after = lax.ppermute(mesh_features, "grid", down)
    out_weight = output_weight.T
    me_spec = pl.BlockSpec(memory_space=pltpu.SMEM)
    in_hbm = pl.BlockSpec(memory_space=pltpu.HBM)
    query, edges_t, src_high, src_low = pl.pallas_call(
        query_kernel,
        in_specs=[me_spec, whole(), in_hbm, in_hbm, in_hbm],
        out_specs=[whole()] * 4,
        out_shape=[
            jax.ShapeDtypeStruct((members, points, width), f32),
            jax.ShapeDtypeStruct((points, 8), jnp.int32),
            jax.ShapeDtypeStruct((width, width), bf16),
            jax.ShapeDtypeStruct((width, width), bf16),
        ],
        scratch_shapes=[
            pltpu.VMEM((members, points, width), f32),
            pltpu.VMEM((width, width), f32),
            pltpu.VMEM((width, width), f32),
            pltpu.SemaphoreType.DMA((2 + 2 * members,)),
        ],
        compiler_params=pltpu.CompilerParams(vmem_limit_bytes=vmem_limit),
        name="query",
        interpret=interpret,
    )(
        me,
        pltpu.with_memory_space_constraint(edges, pltpu.HBM),
        pltpu.with_memory_space_constraint(grid_features, pltpu.HBM),
        pltpu.with_memory_space_constraint(dst_weight, pltpu.HBM),
        pltpu.with_memory_space_constraint(src_weight, pltpu.HBM),
    )

    half = points // 2

    def near(me):
        return me[0] >> 1

    def far(me):
        return 1 - (me[0] >> 1)

    def rows_of(side):
        return pl.BlockSpec((1, half, width), lambda n, me: (n, side(me), 0))

    halves = pl.BlockSpec((1, half, width), lambda n, me: (n, 0, 0))
    half_slopes = pl.BlockSpec((1, 4, half, width), lambda n, me: (n, 0, 0, 0))
    part_shape = jax.ShapeDtypeStruct((members, count_vars, 128), f32)
    half_shape = jax.ShapeDtypeStruct((members, half, width), f32)
    slopes_shape = jax.ShapeDtypeStruct((members, 4, half, width), f32)

    def call(kernel, name, work, in_specs, out_specs, out_shape, scratch=()):
        return pl.pallas_call(
            kernel,
            grid_spec=pltpu.PrefetchScalarGridSpec(
                num_scalar_prefetch=1,
                grid=(members,),
                in_specs=in_specs,
                out_specs=out_specs,
                scratch_shapes=list(scratch),
            ),
            out_shape=out_shape,
            compiler_params=params(1),
            cost_estimate=pl.CostEstimate(
                flops=work, bytes_accessed=4 * members * points * width, transcendentals=0
            ),
            name=name,
            interpret=interpret,
        )

    forward_work = 2 * members * half * width * (4 * 256 + 3 * count_vars + 1024)
    backward_work = 2 * members * half * width * (8 * 256 + 6 * count_vars + 3 * width)
    far_slope, far_summed, part2, part3, nodes = call(
        far_forward_kernel,
        "far_forward",
        forward_work,
        [rows_of(far), pl.BlockSpec((half, 8), lambda n, me: (far(me), 0))] + [whole()] * 6,
        [half_slopes, halves] + [whole()] * 3,
        [slopes_shape, half_shape, part_shape, part_shape]
        + [jax.ShapeDtypeStruct((members, 256, width), bf16)],
    )(me, query, edges_t, before, mesh_features, after, src_high, src_low, out_weight)
    to_peer = [[(i, i ^ k) for i in range(4)] for k in range(4)]
    part2 = lax.ppermute(part2, "member", to_peer[2])
    part3 = lax.ppermute(part3, "member", to_peer[3])
    near_slope, near_summed, part0, part1 = call(
        near_forward_kernel,
        "near_forward",
        forward_work,
        [rows_of(near), pl.BlockSpec((half, 8), lambda n, me: (near(me), 0))] + [whole()] * 2,
        [half_slopes, halves] + [whole()] * 2,
        [slopes_shape, half_shape, part_shape, part_shape],
    )(me, query, edges_t, nodes, out_weight)
    part0, part1, part2, part3 = lax.optimization_barrier((part0, part1, part2, part3))
    part1 = lax.ppermute(part1, "member", to_peer[1])

    *slopes, loss = pl.pallas_call(
        score_kernel,
        grid_spec=pltpu.PrefetchScalarGridSpec(
            num_scalar_prefetch=1,
            grid=(1,),
            in_specs=[whole()] * 4 + [pl.BlockSpec((count_vars, 128), lambda i, me: (0, me[0]))],
            out_specs=[whole()] * 5,
        ),
        out_shape=[part_shape] * 4 + [jax.ShapeDtypeStruct((8, 128), f32)],
        compiler_params=params(1),
        name="score",
        interpret=interpret,
    )(me, part0, part1, part2, part3, targets)

    total_members = lax.axis_size("member") * members
    scale = 1.0 / (total_members * points * slabs) ** 0.5
    loss_scale = 1.0 / (points * slabs * count_vars)
    ext_shape = jax.ShapeDtypeStruct((members, 3 * rows, width), f32)
    out_sum_shape = jax.ShapeDtypeStruct((count_vars, width), f32)
    side = jax.ShapeDtypeStruct((members, rows, width), f32)
    chunks = jax.ShapeDtypeStruct((4, 72, 256), f32)

    def backward_specs(which):
        return [whole()] * 2 + [
            half_slopes,
            halves,
            rows_of(which),
            pl.BlockSpec((4, half), lambda n, me: (0, which(me))),
            whole(),
        ]

    slope1 = lax.ppermute(slopes[1], "member", to_peer[1])
    slope2 = lax.ppermute(slopes[2], "member", to_peer[2])
    slope3 = lax.ppermute(slopes[3], "member", to_peer[3])
    near_grad, near_ext, near_dst, near_out = call(
        near_backward_kernel,
        "near_backward",
        backward_work,
        backward_specs(near),
        [halves] + [whole()] * 3,
        [half_shape, ext_shape, jax.ShapeDtypeStruct((width, width), f32), out_sum_shape],
    )(me, slopes[0], slope1, near_slope, near_summed, grid_features, edges, out_weight)
    slope2, slope3, near_dst = lax.optimization_barrier((slope2, slope3, near_dst))
    far_grad, lower, middle, upper, *parts = call(
        functools.partial(far_backward_kernel, scale, loss_scale),
        "far_backward",
        backward_work,
        backward_specs(far) + [whole()] * 7,
        [halves] + [whole()] * 11,
        [half_shape] + [side] * 3 + [chunks] * 8,
        [pltpu.VMEM((members, 3 * rows, width), f32), pltpu.VMEM((1152, width), f32)],
    )(me, slope2, slope3, far_slope, far_summed, grid_features, edges, out_weight,
      near_ext, near_dst, near_out, loss, before, mesh_features, after)
    grad_query = jnp.where(
        member < 2,
        jnp.concatenate([near_grad, far_grad], axis=1),
        jnp.concatenate([far_grad, near_grad], axis=1),
    )

    keep, away = parts[:4], parts[4:]
    second = jnp.where(straight, place["y"], place["x"])
    swapped = [send(away[k], swap_core) for k in order + (0,)]
    halves = [keep[k] + part for k, part in zip(order, swapped)]
    parts = [send(half, first_axis[k]) for k, half in zip(order, halves)]
    upper, lower, last = lax.optimization_barrier((upper, lower, swapped[3]))
    from_prev = lax.ppermute(upper, "grid", up)
    from_next = lax.ppermute(lower, "grid", down)
    total = tree(keep[0] + last, parts)
    parts = [send(total[k : k + 1], second_axis[k]) for k in order]
    *parts, from_prev, from_next = lax.optimization_barrier((*parts, from_prev, from_next))
    total = tree(total[:1], parts)
    parts = [send(total, along_z[k]) for k in order]
    mesh_grad = jnp.einsum(
        "nru,wu->nrw", middle + from_prev + from_next, src_weight, precision=lax.Precision.HIGH
    )
    *parts, mesh_grad = lax.optimization_barrier((*parts, mesh_grad))
    total = tree(total, parts)
    part = send(total, along_z[4])
    grid_grad = jnp.einsum("npu,wu->npw", grad_query, dst_weight, precision=lax.Precision.HIGH)
    part, grid_grad = lax.optimization_barrier((part, grid_grad))
    total = total + part
    total = placed_at(second, total, [send(total, second_axis[k]) for k in order])
    parts = [total] + [send(total, first_axis[k]) for k in order]
    others = [send(part, swap_core) for part in parts]
    square = jax.ShapeDtypeStruct((width, width), f32)
    src_grad, dst_grad, out_grad, loss = pl.pallas_call(
        finish_kernel,
        grid_spec=pltpu.PrefetchScalarGridSpec(
            num_scalar_prefetch=1,
            grid=(1,),
            in_specs=[whole()] * 8,
            out_specs=[whole()] * 3 + [pl.BlockSpec(memory_space=pltpu.SMEM)],
            scratch_shapes=[pltpu.VMEM((128, width), f32)],
        ),
        out_shape=[square, square, out_sum_shape, jax.ShapeDtypeStruct((1, 1), f32)],
        compiler_params=params(1),
        name="finish",
        interpret=interpret,
    )(me, *parts, *others)
    return loss.reshape(()), grid_grad, mesh_grad, src_grad, dst_grad, out_grad.T


def solution(mesh):
    placed = (
        P("member", "grid", None),
        P("member", "grid", None),
        P(None, "grid"),
        P(None, "grid"),
        P(),
        P(),
        P(),
    )
    return jax.shard_map(
        body,
        mesh=mesh,
        in_specs=placed,
        out_specs=(P(), P("member", "grid", None), P("member", "grid", None), P(), P(), P()),
        check_vma=False,
    )
```

```python
import functools

import jax
import jax.numpy as jnp
from jax import lax
from jax.experimental import pallas as pl
from jax.experimental.pallas import tpu as pltpu
from jax.sharding import PartitionSpec as P

alpha_fair = 0.95
smoothing = 0.1
axes = ("member", "grid")
vmem_limit = 24 * 1024 * 1024
f32 = jnp.float32
bf16 = jnp.bfloat16
interpret = False
node_rows = 32
loss_row = 104


def place_of(member, grid):
    return {
        "core": member & 1,
        "y": ((grid >> 5) << 1) | (member >> 1),
        "z": (grid >> 2) & 7,
        "x": grid & 3,
    }


def role_of(place):
    return place["core"] ^ ((place["x"] ^ place["y"]) & 1)


def exchange(change):
    pairs = []
    for member in range(4):
        for grid in range(64):
            place = place_of(member, grid)
            role, changed = role_of(place), change(place)
            place = {**place, **changed}
            if "core" not in changed:
                place["core"] = role ^ ((place["x"] ^ place["y"]) & 1)
            member_to = ((place["y"] & 1) << 1) | place["core"]
            grid_to = ((place["y"] >> 1) << 5) | (place["z"] << 2) | place["x"]
            pairs.append((member * 64 + grid, member_to * 64 + grid_to))
    return pairs


swap_core = exchange(lambda c: {"core": c["core"] ^ 1})
first_axis = [
    exchange(lambda c, k=k: {"x": c["x"] ^ k} if role_of(c) == 0 else {"y": c["y"] ^ k}) for k in range(4)
]
second_axis = [
    exchange(lambda c, k=k: {"y": c["y"] ^ k} if role_of(c) == 0 else {"x": c["x"] ^ k}) for k in range(4)
]
along_z = [exchange(lambda c, k=k: {"z": c["z"] ^ k}) for k in range(8)]


def send(value, pairs):
    return lax.ppermute(value, axes, pairs)


def split(value):
    high = value.astype(bf16)
    return high, (value - high.astype(f32)).astype(bf16)


def dot3(left, right, dims):
    def one(a, b):
        return lax.dot_general(a, b, (dims, ((), ())), preferred_element_type=f32)

    return one(left[0], right[0]) + (one(left[0], right[1]) + one(left[1], right[0]))


NN = ((1,), (0,))
NT = ((1,), (1,))
TN = ((0,), (0,))


def query_kernel(me, edges, features, weight, src_weight, query, edges_t, src_high, src_low,
                 held, held_weight, held_src, sems):
    members, points = features.shape[0], features.shape[1]
    half = points // 2
    loads = [pltpu.make_async_copy(weight, held_weight, sems.at[0])]
    for i in range(2 * members):
        piece = (i // 2, pl.ds((i % 2) * half, half))
        loads.append(pltpu.make_async_copy(features.at[piece], held.at[piece], sems.at[1 + i]))
    loads.append(pltpu.make_async_copy(src_weight, held_src, sems.at[1 + 2 * members]))
    for load in loads:
        load.start()
    local = edges[...] - (me[1] - 1) * node_rows
    edges_t[...] = jnp.concatenate([local, local], axis=0).T
    loads[0].wait()
    high, low = split(0.5 * held_weight[...])
    for i in range(2 * members):
        loads[1 + i].wait()
        piece = (i // 2, pl.ds((i % 2) * half, half))
        query[piece] = dot3(split(held[piece]), (high, low), NN)
    loads[-1].wait()
    src_high[...], src_low[...] = split(0.5 * held_src[...])


def chunk_rows(width):
    return ((0, 0, 32), (32, width, 32), (64, 2 * width, 8))


def forward(me, member, query, edges, nodes, out_weight, slope, summed, same, flipped):
    points = query.shape[1]
    columns = lax.broadcasted_iota(jnp.int32, (points, 256), 1) & 127
    local = edges[...]
    total = None
    for k in range(4):
        hot = jnp.where(local[:, k : k + 1] == columns, 1.0, 0.0).astype(bf16)
        half = query[0] + jnp.dot(hot, nodes[member], preferred_element_type=f32)
        curve = jnp.tanh(half)
        active = half * curve + half
        curve = 0.5 * curve
        slope[0, k] = (curve + 0.5) + active * (0.5 - curve)
        total = active if total is None else total + active
    summed[0] = total
    fields = dot3(split(out_weight[...]), split(total), NT)
    left, right = fields[:, 0:128], fields[:, 128:256]
    even = (me[0] & 1) == 0
    same[member] = jnp.where(even, left, right)
    flipped[member] = jnp.where(even, right, left)


def far_forward_kernel(me, query, edges, before, own, after, src_high, src_low, out_weight,
                       slope, summed, same, flipped, nodes):
    member = pl.program_id(0)
    rows = own.shape[1]

    @pl.when(member == 0)
    def _():
        nodes[...] = jnp.zeros_like(nodes)
        ext = jnp.concatenate([side[n] for n in range(2) for side in (before, own, after)], axis=0)
        high, low = split(dot3(split(ext), (src_high[...], src_low[...]), NN))
        for n in range(2):
            at = slice(n * 3 * rows, (n + 1) * 3 * rows)
            nodes[n, 0 : 3 * rows] = high[at]
            nodes[n, 128 : 128 + 3 * rows] = low[at]

    forward(me, member, query, edges, nodes, out_weight, slope, summed, same, flipped)


def near_forward_kernel(me, query, edges, nodes, out_weight, slope, summed, same, flipped):
    forward(me, pl.program_id(0), query, edges, nodes, out_weight, slope, summed, same, flipped)


def score_kernel(me, part0, part1, part2, part3, targets, out0, out1, out2, out3, loss):
    parts, outs = (part0, part1, part2, part3), (out0, out1, out2, out3)
    count = 8
    spread = (1.0 - alpha_fair) / count
    factor = (1.0 - spread) / (count * (count - 1))
    rows = targets.shape[0]
    near = jnp.zeros((1, 128), f32)
    far = jnp.zeros((1, 128), f32)
    for start in range(0, rows, 8):
        height = min(8, rows - start)
        at = pl.ds(start, height)
        truth = targets[at]
        fields = [parts[j // 2][j % 2, at] for j in range(count)]
        slopes, dist_sum = [], None
        for field in fields:
            error = field - truth
            square = error * error + smoothing * smoothing
            inverse = lax.rsqrt(square)
            dist = square * inverse
            dist_sum = dist if dist_sum is None else dist_sum + dist
            slopes.append(error * inverse * (1.0 / count))
        pair_sum = None
        pairs = [None] * count
        for j in range(count):
            for k in range(j + 1, count):
                differ = fields[j] - fields[k]
                square = differ * differ + smoothing * smoothing
                inverse = lax.rsqrt(square)
                dist = square * inverse - smoothing
                pair_sum = dist if pair_sum is None else pair_sum + dist
                term = differ * inverse
                pairs[j] = term if pairs[j] is None else pairs[j] + term
                pairs[k] = -term if pairs[k] is None else pairs[k] - term
        near += jnp.sum(dist_sum, axis=0, keepdims=True)
        far += jnp.sum(pair_sum, axis=0, keepdims=True)
        for j in range(count):
            outs[j // 2][j % 2, at] = slopes[j] - factor * pairs[j]
    loss[...] = jnp.broadcast_to(near * (1.0 / count) - factor * far, loss.shape)


def backward(me, member, same, flipped, slope, summed, features, edges, out_weight,
             grad_query, grad_ext, dst_sum, out_sum):
    points = summed.shape[1]
    even = (me[0] & 1) == 0
    one, two = same[member], flipped[member]
    left, right = jnp.where(even, one, two), jnp.where(even, two, one)
    here = split(jnp.concatenate([left, right], axis=1))
    back = dot3(here, split(out_weight[...]), TN)
    out_sum[...] += dot3(here, split(summed[0]), NN)
    local = edges[...] - (me[1] - 1) * node_rows
    nodes = lax.broadcasted_iota(jnp.int32, (3 * node_rows, points), 0)
    scattered = None
    slope_sum = None
    for k in range(4):
        hot = jnp.where(local[k : k + 1] == nodes, 1.0, 0.0).astype(bf16)
        slope_k = slope[0, k]
        slope_sum = slope_k if slope_sum is None else slope_sum + slope_k
        high, low = split(back * slope_k)
        term = jnp.dot(hot, high, preferred_element_type=f32) + jnp.dot(
            hot, low, preferred_element_type=f32
        )
        scattered = term if scattered is None else scattered + term
    grad_ext[member] += scattered
    into_query = back * slope_sum
    grad_query[0] = into_query
    dst_sum[...] += dot3(split(features[0]), split(into_query), TN)


def near_backward_kernel(me, same, flipped, slope, summed, features, edges, out_weight,
                         grad_query, grad_ext, dst_sum, out_sum):
    member = pl.program_id(0)

    @pl.when(member == 0)
    def _():
        for total in (grad_ext, dst_sum, out_sum):
            total[...] = jnp.zeros_like(total)

    backward(me, member, same, flipped, slope, summed, features, edges, out_weight,
             grad_query, grad_ext, dst_sum, out_sum)


def far_backward_kernel(scale, loss_scale, me, same, flipped, slope, summed, features, edges, out_weight,
                        near_ext, near_dst, near_out, loss, before, own, after,
                        grad_query, lower, middle, upper, *rest):
    keep, away, (grad_ext, sums) = rest[:4], rest[4:8], rest[8:]
    member = pl.program_id(0)
    rows = own.shape[1]
    width = features.shape[2]
    count_vars = out_weight.shape[0]
    dst_sum = sums.at[width : 2 * width]
    out_sum = sums.at[2 * width : 2 * width + count_vars]

    @pl.when(member == 0)
    def _():
        sums[2 * width :] = jnp.zeros((sums.shape[0] - 2 * width, width), f32)
        grad_ext[...] = near_ext[...]
        dst_sum[...] = near_dst[...]
        out_sum[...] = near_out[...]

    backward(me, member, same, flipped, slope, summed, features, edges, out_weight,
             grad_query, grad_ext, dst_sum, out_sum)

    @pl.when(member == pl.num_programs(0) - 1)
    def _():
        ext = jnp.concatenate([side[n] for n in range(2) for side in (before, own, after)], axis=0)
        grads = jnp.concatenate([grad_ext[0], grad_ext[1]], axis=0)
        sums[0:width] = dot3(split(ext), split(grads), TN)
        for n in range(2):
            for i, side in enumerate((lower, middle, upper)):
                side[n] = grad_ext[n, i * rows : (i + 1) * rows]
        end = 2 * width + loss_row
        sums[end : end + 8] = jnp.full((8, width), jnp.sum(loss[0:1]) * (loss_scale / scale), f32)
        for j in range(16):
            for out, core, order in ((keep, me[2], me[3]), (away, 1 - me[2], me[4])):
                chunk = j ^ order
                lanes = pl.ds(pl.multiple_of(core * 256, 128), 256)
                for to, start, height in chunk_rows(width):
                    at = pl.ds(pl.multiple_of(start + chunk * height, 8), height)
                    out[j // 4][j % 4, to : to + height] = sums[at, lanes] * scale


def finish_kernel(me, *refs):
    parts, (src_grad, dst_grad, out_grad, loss, rest) = refs[:8], refs[8:]
    width = src_grad.shape[0]
    for i, part in enumerate(parts):
        core, order = (me[2], me[3]) if i < 4 else (1 - me[2], me[4])
        group = (order >> 2) ^ peer_order[i % 4]
        lanes = pl.ds(pl.multiple_of(core * 256, 128), 256)
        for j in range(4):
            for out, (to, _, height) in zip((src_grad, dst_grad, rest), chunk_rows(width)):
                at = pl.ds(pl.multiple_of((group * 4 + j) * height, 8), height)
                out[at, lanes] = part[j, to : to + height]
    out_grad[...] = rest[0 : out_grad.shape[0]]
    loss[0, 0] = jnp.max(rest[loss_row : loss_row + 8, 0:128])


def whole(shape=None):
    return pl.BlockSpec(memory_space=pltpu.VMEM)


def params(dims):
    return pltpu.CompilerParams(dimension_semantics=("arbitrary",) * dims, vmem_limit_bytes=vmem_limit)


order = (2, 1, 3)
peer_order = (0,) + order


def tree(total, parts):
    return (total + parts[0]) + (parts[1] + parts[2])


def placed_at(place, total, parts):
    size = total.shape[0]
    whole_value = jnp.zeros((4 * size,) + total.shape[1:], f32)
    for k, part in zip((0,) + order, [total] + parts):
        whole_value = lax.dynamic_update_slice(whole_value, part, ((place ^ k) * size, 0, 0))
    return whole_value


def body(mesh_features, grid_features, targets, edges, src_weight, dst_weight, output_weight):
    members, rows, width = mesh_features.shape
    points = grid_features.shape[1]
    count_vars = targets.shape[0]
    slabs = lax.axis_size("grid")
    member, grid = lax.axis_index("member"), lax.axis_index("grid")
    place = place_of(member, grid)
    x_then_y = place["x"] * 4 + place["y"]
    y_then_x = place["y"] * 4 + place["x"]
    role = role_of(place)
    straight = role == 0
    me = jnp.stack([
        member,
        grid,
        role,
        jnp.where(straight, x_then_y, y_then_x),
        jnp.where(straight, y_then_x, x_then_y),
    ]).astype(jnp.int32)

    up = [(i, i + 1) for i in range(slabs - 1)]
    down = [(j, i) for i, j in up]
    before = lax.ppermute(mesh_features, "grid", up)
    after = lax.ppermute(mesh_features, "grid", down)
    out_weight = output_weight.T
    me_spec = pl.BlockSpec(memory_space=pltpu.SMEM)
    in_hbm = pl.BlockSpec(memory_space=pltpu.HBM)
    query, edges_t, src_high, src_low = pl.pallas_call(
        query_kernel,
        in_specs=[me_spec, whole(), in_hbm, in_hbm, in_hbm],
        out_specs=[whole()] * 4,
        out_shape=[
            jax.ShapeDtypeStruct((members, points, width), f32),
            jax.ShapeDtypeStruct((points, 8), jnp.int32),
            jax.ShapeDtypeStruct((width, width), bf16),
            jax.ShapeDtypeStruct((width, width), bf16),
        ],
        scratch_shapes=[
            pltpu.VMEM((members, points, width), f32),
            pltpu.VMEM((width, width), f32),
            pltpu.VMEM((width, width), f32),
            pltpu.SemaphoreType.DMA((2 + 2 * members,)),
        ],
        compiler_params=pltpu.CompilerParams(vmem_limit_bytes=vmem_limit),
        name="query",
        interpret=interpret,
    )(
        me,
        pltpu.with_memory_space_constraint(edges, pltpu.HBM),
        pltpu.with_memory_space_constraint(grid_features, pltpu.HBM),
        pltpu.with_memory_space_constraint(dst_weight, pltpu.HBM),
        pltpu.with_memory_space_constraint(src_weight, pltpu.HBM),
    )

    half = points // 2

    def near(me):
        return me[0] >> 1

    def far(me):
        return 1 - (me[0] >> 1)

    def rows_of(side):
        return pl.BlockSpec((1, half, width), lambda n, me: (n, side(me), 0))

    halves = pl.BlockSpec((1, half, width), lambda n, me: (n, 0, 0))
    half_slopes = pl.BlockSpec((1, 4, half, width), lambda n, me: (n, 0, 0, 0))
    part_shape = jax.ShapeDtypeStruct((members, count_vars, 128), f32)
    half_shape = jax.ShapeDtypeStruct((members, half, width), f32)
    slopes_shape = jax.ShapeDtypeStruct((members, 4, half, width), f32)

    def call(kernel, name, work, in_specs, out_specs, out_shape, scratch=()):
        return pl.pallas_call(
            kernel,
            grid_spec=pltpu.PrefetchScalarGridSpec(
                num_scalar_prefetch=1,
                grid=(members,),
                in_specs=in_specs,
                out_specs=out_specs,
                scratch_shapes=list(scratch),
            ),
            out_shape=out_shape,
            compiler_params=params(1),
            cost_estimate=pl.CostEstimate(
                flops=work, bytes_accessed=4 * members * points * width, transcendentals=0
            ),
            name=name,
            interpret=interpret,
        )

    forward_work = 2 * members * half * width * (4 * 256 + 3 * count_vars + 1024)
    backward_work = 2 * members * half * width * (8 * 256 + 6 * count_vars + 3 * width)
    far_slope, far_summed, part2, part3, nodes = call(
        far_forward_kernel,
        "far_forward",
        forward_work,
        [rows_of(far), pl.BlockSpec((half, 8), lambda n, me: (far(me), 0))] + [whole()] * 6,
        [half_slopes, halves] + [whole()] * 3,
        [slopes_shape, half_shape, part_shape, part_shape]
        + [jax.ShapeDtypeStruct((members, 256, width), bf16)],
    )(me, query, edges_t, before, mesh_features, after, src_high, src_low, out_weight)
    to_peer = [[(i, i ^ k) for i in range(4)] for k in range(4)]
    part2 = lax.ppermute(part2, "member", to_peer[2])
    part3 = lax.ppermute(part3, "member", to_peer[3])
    near_slope, near_summed, part0, part1 = call(
        near_forward_kernel,
        "near_forward",
        forward_work,
        [rows_of(near), pl.BlockSpec((half, 8), lambda n, me: (near(me), 0))] + [whole()] * 2,
        [half_slopes, halves] + [whole()] * 2,
        [slopes_shape, half_shape, part_shape, part_shape],
    )(me, query, edges_t, nodes, out_weight)
    part0, part1, part2, part3 = lax.optimization_barrier((part0, part1, part2, part3))
    part1 = lax.ppermute(part1, "member", to_peer[1])

    *slopes, loss = pl.pallas_call(
        score_kernel,
        grid_spec=pltpu.PrefetchScalarGridSpec(
            num_scalar_prefetch=1,
            grid=(1,),
            in_specs=[whole()] * 4 + [pl.BlockSpec((count_vars, 128), lambda i, me: (0, me[0]))],
            out_specs=[whole()] * 5,
        ),
        out_shape=[part_shape] * 4 + [jax.ShapeDtypeStruct((8, 128), f32)],
        compiler_params=params(1),
        name="score",
        interpret=interpret,
    )(me, part0, part1, part2, part3, targets)

    total_members = lax.axis_size("member") * members
    scale = 1.0 / (total_members * points * slabs) ** 0.5
    loss_scale = 1.0 / (points * slabs * count_vars)
    ext_shape = jax.ShapeDtypeStruct((members, 3 * rows, width), f32)
    out_sum_shape = jax.ShapeDtypeStruct((count_vars, width), f32)
    side = jax.ShapeDtypeStruct((members, rows, width), f32)
    chunks = jax.ShapeDtypeStruct((4, 72, 256), f32)

    def backward_specs(which):
        return [whole()] * 2 + [
            half_slopes,
            halves,
            rows_of(which),
            pl.BlockSpec((4, half), lambda n, me: (0, which(me))),
            whole(),
        ]

    slope1 = lax.ppermute(slopes[1], "member", to_peer[1])
    slope2 = lax.ppermute(slopes[2], "member", to_peer[2])
    slope3 = lax.ppermute(slopes[3], "member", to_peer[3])
    near_grad, near_ext, near_dst, near_out = call(
        near_backward_kernel,
        "near_backward",
        backward_work,
        backward_specs(near),
        [halves] + [whole()] * 3,
        [half_shape, ext_shape, jax.ShapeDtypeStruct((width, width), f32), out_sum_shape],
    )(me, slopes[0], slope1, near_slope, near_summed, grid_features, edges, out_weight)
    slope2, slope3, near_dst = lax.optimization_barrier((slope2, slope3, near_dst))
    far_grad, lower, middle, upper, *parts = call(
        functools.partial(far_backward_kernel, scale, loss_scale),
        "far_backward",
        backward_work,
        backward_specs(far) + [whole()] * 7,
        [halves] + [whole()] * 11,
        [half_shape] + [side] * 3 + [chunks] * 8,
        [pltpu.VMEM((members, 3 * rows, width), f32), pltpu.VMEM((1152, width), f32)],
    )(me, slope2, slope3, far_slope, far_summed, grid_features, edges, out_weight,
      near_ext, near_dst, near_out, loss, before, mesh_features, after)
    grad_query = jnp.where(
        member < 2,
        jnp.concatenate([near_grad, far_grad], axis=1),
        jnp.concatenate([far_grad, near_grad], axis=1),
    )

    keep, away = parts[:4], parts[4:]
    second = jnp.where(straight, place["y"], place["x"])
    swapped = [send(away[k], swap_core) for k in order + (0,)]
    halves = [keep[k] + part for k, part in zip(order, swapped)]
    parts = [send(half, first_axis[k]) for k, half in zip(order, halves)]
    upper, lower, last = lax.optimization_barrier((upper, lower, swapped[3]))
    from_prev = lax.ppermute(upper, "grid", up)
    from_next = lax.ppermute(lower, "grid", down)
    total = tree(keep[0] + last, parts)
    parts = [send(total[k : k + 1], second_axis[k]) for k in order]
    *parts, from_prev, from_next = lax.optimization_barrier((*parts, from_prev, from_next))
    total = tree(total[:1], parts)
    parts = [send(total, along_z[k]) for k in order]
    mesh_grad = jnp.einsum(
        "nru,wu->nrw", middle + from_prev + from_next, src_weight, precision=lax.Precision.HIGH
    )
    *parts, mesh_grad = lax.optimization_barrier((*parts, mesh_grad))
    total = tree(total, parts)
    part = send(total, along_z[4])
    grid_grad = jnp.einsum("npu,wu->npw", grad_query, dst_weight, precision=lax.Precision.HIGH)
    part, grid_grad = lax.optimization_barrier((part, grid_grad))
    total = total + part
    total = placed_at(second, total, [send(total, second_axis[k]) for k in order])
    parts = [total] + [send(total, first_axis[k]) for k in order]
    others = [send(part, swap_core) for part in parts]
    square = jax.ShapeDtypeStruct((width, width), f32)
    src_grad, dst_grad, out_grad, loss = pl.pallas_call(
        finish_kernel,
        grid_spec=pltpu.PrefetchScalarGridSpec(
            num_scalar_prefetch=1,
            grid=(1,),
            in_specs=[whole()] * 8,
            out_specs=[whole()] * 3 + [pl.BlockSpec(memory_space=pltpu.SMEM)],
            scratch_shapes=[pltpu.VMEM((128, width), f32)],
        ),
        out_shape=[square, square, out_sum_shape, jax.ShapeDtypeStruct((1, 1), f32)],
        compiler_params=params(1),
        name="finish",
        interpret=interpret,
    )(me, *parts, *others)
    return loss.reshape(()), grid_grad, mesh_grad, src_grad, dst_grad, out_grad.T


def solution(mesh):
    placed = (
        P("member", "grid", None),
        P("member", "grid", None),
        P(None, "grid"),
        P(None, "grid"),
        P(),
        P(),
        P(),
    )
    return jax.shard_map(
        body,
        mesh=mesh,
        in_specs=placed,
        out_specs=(P(), P("member", "grid", None), P("member", "grid", None), P(), P(), P()),
        check_vma=False,
    )
```

```python
import functools

import jax
import jax.numpy as jnp
from jax import lax
from jax.experimental import pallas as pl
from jax.experimental.pallas import tpu as pltpu
from jax.sharding import PartitionSpec as P

alpha_fair = 0.95
smoothing = 0.1
axes = ("member", "grid")
vmem_limit = 24 * 1024 * 1024
f32 = jnp.float32
bf16 = jnp.bfloat16
interpret = False
node_rows = 32
loss_row = 104


def place_of(member, grid):
    return {
        "core": member & 1,
        "y": ((grid >> 5) << 1) | (member >> 1),
        "z": (grid >> 2) & 7,
        "x": grid & 3,
    }


def role_of(place):
    return place["core"] ^ ((place["x"] ^ place["y"]) & 1)


def exchange(change):
    pairs = []
    for member in range(4):
        for grid in range(64):
            place = place_of(member, grid)
            role, changed = role_of(place), change(place)
            place = {**place, **changed}
            if "core" not in changed:
                place["core"] = role ^ ((place["x"] ^ place["y"]) & 1)
            member_to = ((place["y"] & 1) << 1) | place["core"]
            grid_to = ((place["y"] >> 1) << 5) | (place["z"] << 2) | place["x"]
            pairs.append((member * 64 + grid, member_to * 64 + grid_to))
    return pairs


swap_core = exchange(lambda c: {"core": c["core"] ^ 1})
first_axis = [
    exchange(lambda c, k=k: {"x": c["x"] ^ k} if role_of(c) == 0 else {"y": c["y"] ^ k}) for k in range(4)
]
second_axis = [
    exchange(lambda c, k=k: {"y": c["y"] ^ k} if role_of(c) == 0 else {"x": c["x"] ^ k}) for k in range(4)
]
along_z = [exchange(lambda c, k=k: {"z": c["z"] ^ k}) for k in range(8)]


def send(value, pairs):
    return lax.ppermute(value, axes, pairs)


def split(value):
    high = value.astype(bf16)
    return high, (value - high.astype(f32)).astype(bf16)


def dot3(left, right, dims):
    def one(a, b):
        return lax.dot_general(a, b, (dims, ((), ())), preferred_element_type=f32)

    return one(left[0], right[0]) + (one(left[0], right[1]) + one(left[1], right[0]))


NN = ((1,), (0,))
NT = ((1,), (1,))
TN = ((0,), (0,))


def query_kernel(me, edges, features, weight, src_weight, query, edges_t, src_high, src_low,
                 held, held_weight, held_src, sems):
    members, points = features.shape[0], features.shape[1]
    half = points // 2
    loads = [pltpu.make_async_copy(weight, held_weight, sems.at[0])]
    for i in range(2 * members):
        piece = (i // 2, pl.ds((i % 2) * half, half))
        loads.append(pltpu.make_async_copy(features.at[piece], held.at[piece], sems.at[1 + i]))
    loads.append(pltpu.make_async_copy(src_weight, held_src, sems.at[1 + 2 * members]))
    for load in loads:
        load.start()
    local = edges[...] - (me[1] - 1) * node_rows
    edges_t[...] = jnp.concatenate([local, local], axis=0).T
    loads[0].wait()
    high, low = split(0.5 * held_weight[...])
    for i in range(2 * members):
        loads[1 + i].wait()
        piece = (i // 2, pl.ds((i % 2) * half, half))
        query[piece] = dot3(split(held[piece]), (high, low), NN)
    loads[-1].wait()
    src_high[...], src_low[...] = split(0.5 * held_src[...])


def chunk_rows(width):
    return ((0, 0, 32), (32, width, 32), (64, 2 * width, 8))


def forward(me, member, query, edges, nodes, out_weight, slope, summed, same, flipped):
    points = query.shape[1]
    columns = lax.broadcasted_iota(jnp.int32, (points, 256), 1) & 127
    local = edges[...]
    total = None
    for k in range(4):
        hot = jnp.where(local[:, k : k + 1] == columns, 1.0, 0.0).astype(bf16)
        half = query[0] + jnp.dot(hot, nodes[member], preferred_element_type=f32)
        curve = jnp.tanh(half)
        active = half * curve + half
        curve = 0.5 * curve
        slope[0, k] = (curve + 0.5) + active * (0.5 - curve)
        total = active if total is None else total + active
    summed[0] = total
    fields = dot3(split(out_weight[...]), split(total), NT)
    left, right = fields[:, 0:128], fields[:, 128:256]
    even = (me[0] & 1) == 0
    same[member] = jnp.where(even, left, right)
    flipped[member] = jnp.where(even, right, left)


def extended(me, one, own, two):
    even = (me[1] & 1) == 0
    rows = []
    for n in range(own.shape[0]):
        rows += [jnp.where(even, two[n], one[n]), own[n], jnp.where(even, one[n], two[n])]
    return jnp.concatenate(rows, axis=0)


def far_forward_kernel(me, query, edges, one, own, two, src_high, src_low, out_weight,
                       slope, summed, same, flipped, nodes):
    member = pl.program_id(0)
    rows = own.shape[1]

    @pl.when(member == 0)
    def _():
        nodes[...] = jnp.zeros_like(nodes)
        ext = extended(me, one, own, two)
        high, low = split(dot3(split(ext), (src_high[...], src_low[...]), NN))
        for n in range(2):
            at = slice(n * 3 * rows, (n + 1) * 3 * rows)
            nodes[n, 0 : 3 * rows] = high[at]
            nodes[n, 128 : 128 + 3 * rows] = low[at]

    forward(me, member, query, edges, nodes, out_weight, slope, summed, same, flipped)


def near_forward_kernel(me, query, edges, nodes, out_weight, slope, summed, same, flipped):
    forward(me, pl.program_id(0), query, edges, nodes, out_weight, slope, summed, same, flipped)


def score_kernel(me, part0, part1, part2, part3, targets, out0, out1, out2, out3, loss):
    parts, outs = (part0, part1, part2, part3), (out0, out1, out2, out3)
    count = 8
    spread = (1.0 - alpha_fair) / count
    factor = (1.0 - spread) / (count * (count - 1))
    rows = targets.shape[0]
    near = jnp.zeros((1, 128), f32)
    far = jnp.zeros((1, 128), f32)
    for start in range(0, rows, 8):
        height = min(8, rows - start)
        at = pl.ds(start, height)
        truth = targets[at]
        fields = [parts[j // 2][j % 2, at] for j in range(count)]
        slopes, dist_sum = [], None
        for field in fields:
            error = field - truth
            square = error * error + smoothing * smoothing
            inverse = lax.rsqrt(square)
            dist = square * inverse
            dist_sum = dist if dist_sum is None else dist_sum + dist
            slopes.append(error * inverse * (1.0 / count))
        pair_sum = None
        pairs = [None] * count
        for j in range(count):
            for k in range(j + 1, count):
                differ = fields[j] - fields[k]
                square = differ * differ + smoothing * smoothing
                inverse = lax.rsqrt(square)
                dist = square * inverse - smoothing
                pair_sum = dist if pair_sum is None else pair_sum + dist
                term = differ * inverse
                pairs[j] = term if pairs[j] is None else pairs[j] + term
                pairs[k] = -term if pairs[k] is None else pairs[k] - term
        near += jnp.sum(dist_sum, axis=0, keepdims=True)
        far += jnp.sum(pair_sum, axis=0, keepdims=True)
        for j in range(count):
            outs[j // 2][j % 2, at] = slopes[j] - factor * pairs[j]
    loss[...] = jnp.broadcast_to(near * (1.0 / count) - factor * far, loss.shape)


def backward(me, member, same, flipped, slope, summed, features, edges, out_weight,
             grad_query, grad_ext, dst_sum, out_sum):
    points = summed.shape[1]
    even = (me[0] & 1) == 0
    one, two = same[member], flipped[member]
    left, right = jnp.where(even, one, two), jnp.where(even, two, one)
    here = split(jnp.concatenate([left, right], axis=1))
    back = dot3(here, split(out_weight[...]), TN)
    out_sum[...] += dot3(here, split(summed[0]), NN)
    local = edges[...] - (me[1] - 1) * node_rows
    nodes = lax.broadcasted_iota(jnp.int32, (3 * node_rows, points), 0)
    scattered = None
    slope_sum = None
    for k in range(4):
        hot = jnp.where(local[k : k + 1] == nodes, 1.0, 0.0).astype(bf16)
        slope_k = slope[0, k]
        slope_sum = slope_k if slope_sum is None else slope_sum + slope_k
        high, low = split(back * slope_k)
        term = jnp.dot(hot, high, preferred_element_type=f32) + jnp.dot(
            hot, low, preferred_element_type=f32
        )
        scattered = term if scattered is None else scattered + term
    grad_ext[member] += scattered
    into_query = back * slope_sum
    grad_query[0] = into_query
    dst_sum[...] += dot3(split(features[0]), split(into_query), TN)


def near_backward_kernel(me, same, flipped, slope, summed, features, edges, out_weight,
                         grad_query, grad_ext, dst_sum, out_sum):
    member = pl.program_id(0)

    @pl.when(member == 0)
    def _():
        for total in (grad_ext, dst_sum, out_sum):
            total[...] = jnp.zeros_like(total)

    backward(me, member, same, flipped, slope, summed, features, edges, out_weight,
             grad_query, grad_ext, dst_sum, out_sum)


def far_backward_kernel(scale, loss_scale, me, same, flipped, slope, summed, features, edges, out_weight,
                        near_ext, near_dst, near_out, loss, one, own, two,
                        grad_query, to_one, middle, to_two, *rest):
    keep, away, (grad_ext, sums) = rest[:4], rest[4:8], rest[8:]
    member = pl.program_id(0)
    rows = own.shape[1]
    width = features.shape[2]
    count_vars = out_weight.shape[0]
    dst_sum = sums.at[width : 2 * width]
    out_sum = sums.at[2 * width : 2 * width + count_vars]

    @pl.when(member == 0)
    def _():
        sums[2 * width :] = jnp.zeros((sums.shape[0] - 2 * width, width), f32)
        grad_ext[...] = near_ext[...]
        dst_sum[...] = near_dst[...]
        out_sum[...] = near_out[...]

    backward(me, member, same, flipped, slope, summed, features, edges, out_weight,
             grad_query, grad_ext, dst_sum, out_sum)

    @pl.when(member == pl.num_programs(0) - 1)
    def _():
        ext = extended(me, one, own, two)
        grads = jnp.concatenate([grad_ext[0], grad_ext[1]], axis=0)
        sums[0:width] = dot3(split(ext), split(grads), TN)
        even = (me[1] & 1) == 0
        for n in range(2):
            lower, upper = grad_ext[n, 0:rows], grad_ext[n, 2 * rows : 3 * rows]
            to_one[n] = jnp.where(even, upper, lower)
            to_two[n] = jnp.where(even, lower, upper)
            middle[n] = grad_ext[n, rows : 2 * rows]
        end = 2 * width + loss_row
        sums[end : end + 8] = jnp.full((8, width), jnp.sum(loss[0:1]) * (loss_scale / scale), f32)
        for j in range(16):
            for out, core, order in ((keep, me[2], me[3]), (away, 1 - me[2], me[4])):
                chunk = j ^ order
                lanes = pl.ds(pl.multiple_of(core * 256, 128), 256)
                for to, start, height in chunk_rows(width):
                    at = pl.ds(pl.multiple_of(start + chunk * height, 8), height)
                    out[j // 4][j % 4, to : to + height] = sums[at, lanes] * scale


def finish_kernel(me, *refs):
    parts, (src_grad, dst_grad, out_grad, loss, rest) = refs[:8], refs[8:]
    width = src_grad.shape[0]
    for i, part in enumerate(parts):
        core, order = (me[2], me[3]) if i < 4 else (1 - me[2], me[4])
        group = (order >> 2) ^ peer_order[i % 4]
        lanes = pl.ds(pl.multiple_of(core * 256, 128), 256)
        for j in range(4):
            for out, (to, _, height) in zip((src_grad, dst_grad, rest), chunk_rows(width)):
                at = pl.ds(pl.multiple_of((group * 4 + j) * height, 8), height)
                out[at, lanes] = part[j, to : to + height]
    out_grad[...] = rest[0 : out_grad.shape[0]]
    loss[0, 0] = jnp.max(rest[loss_row : loss_row + 8, 0:128])


def whole(shape=None):
    return pl.BlockSpec(memory_space=pltpu.VMEM)


def params(dims):
    return pltpu.CompilerParams(dimension_semantics=("arbitrary",) * dims, vmem_limit_bytes=vmem_limit)


order = (2, 1, 3)
peer_order = (0,) + order


def tree(total, parts):
    return (total + parts[0]) + (parts[1] + parts[2])


def placed_at(place, total, parts):
    size = total.shape[0]
    whole_value = jnp.zeros((4 * size,) + total.shape[1:], f32)
    for k, part in zip((0,) + order, [total] + parts):
        whole_value = lax.dynamic_update_slice(whole_value, part, ((place ^ k) * size, 0, 0))
    return whole_value


def body(mesh_features, grid_features, targets, edges, src_weight, dst_weight, output_weight):
    members, rows, width = mesh_features.shape
    points = grid_features.shape[1]
    count_vars = targets.shape[0]
    slabs = lax.axis_size("grid")
    member, grid = lax.axis_index("member"), lax.axis_index("grid")
    place = place_of(member, grid)
    x_then_y = place["x"] * 4 + place["y"]
    y_then_x = place["y"] * 4 + place["x"]
    role = role_of(place)
    straight = role == 0
    me = jnp.stack([
        member,
        grid,
        role,
        jnp.where(straight, x_then_y, y_then_x),
        jnp.where(straight, y_then_x, x_then_y),
    ]).astype(jnp.int32)

    even_pairs = [(i, i ^ 1) for i in range(slabs)]
    odd_pairs = [(i, i + 1) for i in range(1, slabs - 1, 2)]
    odd_pairs += [(j, i) for i, j in odd_pairs]
    one = lax.ppermute(mesh_features, "grid", even_pairs)
    two = lax.ppermute(mesh_features, "grid", odd_pairs)
    out_weight = output_weight.T
    me_spec = pl.BlockSpec(memory_space=pltpu.SMEM)
    in_hbm = pl.BlockSpec(memory_space=pltpu.HBM)
    query, edges_t, src_high, src_low = pl.pallas_call(
        query_kernel,
        in_specs=[me_spec, whole(), in_hbm, in_hbm, in_hbm],
        out_specs=[whole()] * 4,
        out_shape=[
            jax.ShapeDtypeStruct((members, points, width), f32),
            jax.ShapeDtypeStruct((points, 8), jnp.int32),
            jax.ShapeDtypeStruct((width, width), bf16),
            jax.ShapeDtypeStruct((width, width), bf16),
        ],
        scratch_shapes=[
            pltpu.VMEM((members, points, width), f32),
            pltpu.VMEM((width, width), f32),
            pltpu.VMEM((width, width), f32),
            pltpu.SemaphoreType.DMA((2 + 2 * members,)),
        ],
        compiler_params=pltpu.CompilerParams(vmem_limit_bytes=vmem_limit),
        name="query",
        interpret=interpret,
    )(
        me,
        pltpu.with_memory_space_constraint(edges, pltpu.HBM),
        pltpu.with_memory_space_constraint(grid_features, pltpu.HBM),
        pltpu.with_memory_space_constraint(dst_weight, pltpu.HBM),
        pltpu.with_memory_space_constraint(src_weight, pltpu.HBM),
    )

    half = points // 2

    def near(me):
        return me[0] >> 1

    def far(me):
        return 1 - (me[0] >> 1)

    def rows_of(side):
        return pl.BlockSpec((1, half, width), lambda n, me: (n, side(me), 0))

    halves = pl.BlockSpec((1, half, width), lambda n, me: (n, 0, 0))
    half_slopes = pl.BlockSpec((1, 4, half, width), lambda n, me: (n, 0, 0, 0))
    part_shape = jax.ShapeDtypeStruct((members, count_vars, 128), f32)
    half_shape = jax.ShapeDtypeStruct((members, half, width), f32)
    slopes_shape = jax.ShapeDtypeStruct((members, 4, half, width), f32)

    def call(kernel, name, work, in_specs, out_specs, out_shape, scratch=()):
        return pl.pallas_call(
            kernel,
            grid_spec=pltpu.PrefetchScalarGridSpec(
                num_scalar_prefetch=1,
                grid=(members,),
                in_specs=in_specs,
                out_specs=out_specs,
                scratch_shapes=list(scratch),
            ),
            out_shape=out_shape,
            compiler_params=params(1),
            cost_estimate=pl.CostEstimate(
                flops=work, bytes_accessed=4 * members * points * width, transcendentals=0
            ),
            name=name,
            interpret=interpret,
        )

    forward_work = 2 * members * half * width * (4 * 256 + 3 * count_vars + 1024)
    backward_work = 2 * members * half * width * (8 * 256 + 6 * count_vars + 3 * width)
    far_slope, far_summed, part2, part3, nodes = call(
        far_forward_kernel,
        "far_forward",
        forward_work,
        [rows_of(far), pl.BlockSpec((half, 8), lambda n, me: (far(me), 0))] + [whole()] * 6,
        [half_slopes, halves] + [whole()] * 3,
        [slopes_shape, half_shape, part_shape, part_shape]
        + [jax.ShapeDtypeStruct((members, 256, width), bf16)],
    )(me, query, edges_t, one, mesh_features, two, src_high, src_low, out_weight)
    to_peer = [[(i, i ^ k) for i in range(4)] for k in range(4)]
    part2 = lax.ppermute(part2, "member", to_peer[2])
    part3 = lax.ppermute(part3, "member", to_peer[3])
    near_slope, near_summed, part0, part1 = call(
        near_forward_kernel,
        "near_forward",
        forward_work,
        [rows_of(near), pl.BlockSpec((half, 8), lambda n, me: (near(me), 0))] + [whole()] * 2,
        [half_slopes, halves] + [whole()] * 2,
        [slopes_shape, half_shape, part_shape, part_shape],
    )(me, query, edges_t, nodes, out_weight)
    part0, part1, part2, part3 = lax.optimization_barrier((part0, part1, part2, part3))
    part1 = lax.ppermute(part1, "member", to_peer[1])

    *slopes, loss = pl.pallas_call(
        score_kernel,
        grid_spec=pltpu.PrefetchScalarGridSpec(
            num_scalar_prefetch=1,
            grid=(1,),
            in_specs=[whole()] * 4 + [pl.BlockSpec((count_vars, 128), lambda i, me: (0, me[0]))],
            out_specs=[whole()] * 5,
        ),
        out_shape=[part_shape] * 4 + [jax.ShapeDtypeStruct((8, 128), f32)],
        compiler_params=params(1),
        name="score",
        interpret=interpret,
    )(me, part0, part1, part2, part3, targets)

    total_members = lax.axis_size("member") * members
    scale = 1.0 / (total_members * points * slabs) ** 0.5
    loss_scale = 1.0 / (points * slabs * count_vars)
    ext_shape = jax.ShapeDtypeStruct((members, 3 * rows, width), f32)
    out_sum_shape = jax.ShapeDtypeStruct((count_vars, width), f32)
    side = jax.ShapeDtypeStruct((members, rows, width), f32)
    chunks = jax.ShapeDtypeStruct((4, 72, 256), f32)

    def backward_specs(which):
        return [whole()] * 2 + [
            half_slopes,
            halves,
            rows_of(which),
            pl.BlockSpec((4, half), lambda n, me: (0, which(me))),
            whole(),
        ]

    slope1 = lax.ppermute(slopes[1], "member", to_peer[1])
    slope2 = lax.ppermute(slopes[2], "member", to_peer[2])
    slope3 = lax.ppermute(slopes[3], "member", to_peer[3])
    near_grad, near_ext, near_dst, near_out = call(
        near_backward_kernel,
        "near_backward",
        backward_work,
        backward_specs(near),
        [halves] + [whole()] * 3,
        [half_shape, ext_shape, jax.ShapeDtypeStruct((width, width), f32), out_sum_shape],
    )(me, slopes[0], slope1, near_slope, near_summed, grid_features, edges, out_weight)
    slope2, slope3, near_dst = lax.optimization_barrier((slope2, slope3, near_dst))
    far_grad, to_one, middle, to_two, *parts = call(
        functools.partial(far_backward_kernel, scale, loss_scale),
        "far_backward",
        backward_work,
        backward_specs(far) + [whole()] * 7,
        [halves] + [whole()] * 11,
        [half_shape] + [side] * 3 + [chunks] * 8,
        [pltpu.VMEM((members, 3 * rows, width), f32), pltpu.VMEM((1152, width), f32)],
    )(me, slope2, slope3, far_slope, far_summed, grid_features, edges, out_weight,
      near_ext, near_dst, near_out, loss, one, mesh_features, two)
    grad_query = jnp.where(
        member < 2,
        jnp.concatenate([near_grad, far_grad], axis=1),
        jnp.concatenate([far_grad, near_grad], axis=1),
    )

    keep, away = parts[:4], parts[4:]
    second = jnp.where(straight, place["y"], place["x"])
    swapped = [send(away[k], swap_core) for k in order + (0,)]
    halves = [keep[k] + part for k, part in zip(order, swapped)]
    parts = [send(half, first_axis[k]) for k, half in zip(order, halves)]
    to_one, last = lax.optimization_barrier((to_one, swapped[3]))
    from_one = lax.ppermute(to_one, "grid", even_pairs)
    total = tree(keep[0] + last, parts)
    parts = [send(total[k : k + 1], second_axis[k]) for k in order]
    parts[0], from_one, to_two = lax.optimization_barrier((parts[0], from_one, to_two))
    from_two = lax.ppermute(to_two, "grid", odd_pairs)
    total = tree(total[:1], parts)
    parts = [send(total, along_z[k]) for k in order]
    mesh_grad = jnp.einsum(
        "nru,wu->nrw", middle + from_one + from_two, src_weight, precision=lax.Precision.HIGH
    )
    *parts, mesh_grad = lax.optimization_barrier((*parts, mesh_grad))
    total = tree(total, parts)
    part = send(total, along_z[4])
    grid_grad = jnp.einsum("npu,wu->npw", grad_query, dst_weight, precision=lax.Precision.HIGH)
    part, grid_grad = lax.optimization_barrier((part, grid_grad))
    total = total + part
    total = placed_at(second, total, [send(total, second_axis[k]) for k in order])
    parts = [total] + [send(total, first_axis[k]) for k in order]
    others = [send(part, swap_core) for part in parts]
    square = jax.ShapeDtypeStruct((width, width), f32)
    src_grad, dst_grad, out_grad, loss = pl.pallas_call(
        finish_kernel,
        grid_spec=pltpu.PrefetchScalarGridSpec(
            num_scalar_prefetch=1,
            grid=(1,),
            in_specs=[whole()] * 8,
            out_specs=[whole()] * 3 + [pl.BlockSpec(memory_space=pltpu.SMEM)],
            scratch_shapes=[pltpu.VMEM((128, width), f32)],
        ),
        out_shape=[square, square, out_sum_shape, jax.ShapeDtypeStruct((1, 1), f32)],
        compiler_params=params(1),
        name="finish",
        interpret=interpret,
    )(me, *parts, *others)
    return loss.reshape(()), grid_grad, mesh_grad, src_grad, dst_grad, out_grad.T


def solution(mesh):
    placed = (
        P("member", "grid", None),
        P("member", "grid", None),
        P(None, "grid"),
        P(None, "grid"),
        P(),
        P(),
        P(),
    )
    return jax.shard_map(
        body,
        mesh=mesh,
        in_specs=placed,
        out_specs=(P(), P("member", "grid", None), P("member", "grid", None), P(), P(), P()),
        check_vma=False,
    )
```
